256 devices in a mesh: node: 32 (over x, z), local: 8 (over y, core).
Axes of the slice: x: 4, y: 4, z: 8, core: 2. Of those that a mesh axis runs over, the one named last changes fastest.
Arguments:
- hidden_in: bfloat16 [16384, 2048], P(('node', 'local')), may hold values from -6 to 6
- queries: bfloat16 [16384, 2048], P('node', 'local'), may hold values from -6 to 6
- key_vectors: bfloat16 [16384, 2048], P('node', 'local'), may hold values from -6 to 6
- values: bfloat16 [16384, 4096], P('node', 'local'), may hold values from -6 to 6
- out_gate: bfloat16 [16384, 4096], P('node', 'local'), may hold values from -6 to 6
- log_decay: float32 [16384, 32], P('node', 'local'), may hold values from -1 to 0
- write_rate: float32 [16384, 32], P('node', 'local'), may hold values from 0 to 1
- norm_gain: float32 [128], replicated, may hold values from 0.5 to 1.5
- out_weight: bfloat16 [4096, 2048], P('local'), may hold values from -0.09375 to 0.09375
- post_gain: float32 [2048], replicated, may hold values from 0.5 to 1.5
- expert_index: int32 [16384, 10], P('node'), may hold values from 0 to 255, all different within a row; in each aligned block of 512 rows (0 to 511, 512 to 1023, ...) at most 24 rows name the same one
- route_weight: float32 [16384, 10], P('node'), may hold values from 0.05 to 0.5
- expert_gate_up: bfloat16 [256, 2048, 1024], P(('node', 'local')), may hold values from -0.125 to 0.125
- expert_down: bfloat16 [256, 512, 2048], P(('node', 'local')), may hold values from -0.25 to 0.25
Outputs:
- layer_out: bfloat16 [16384, 2048], P(('node', 'local'))
The draws below stay inside these ranges and needn't reach their ends.
Inputs may be any that keep to these rules, and one draw needn't show every extreme that they name: `expert_index`: each row names 10 different experts; within each aligned block of 512 rows no expert is named by more than 24 rows.
All inputs are finite; a program needn't handle non-finite values.
Results may differ from the reference program's by a relative error of at most 0.018.
Values may be sent and summed in bfloat16 or wider, within the bound.
No kernel may reach another device: no remote copies, remote signals or barrier semaphores. Data moves between devices by JAX's collectives and lax.ppermute only.
A program may use at most 128 MiB of HBM per device.

```python
import math
import jax
import jax.numpy as jnp
import numpy as np
from jax import lax

D = 2048
VALUE_HEADS = 32
HK = 16
DK = 128
DV = 128
FFE = 512
TOP = 10
TOK_NODE = 512
BLOCK = 64
EXP_DEV = 1
SEQUENCE_TOKENS = 16384
EXPERTS = 256
HV_DEV = 4
CAP = 24
N_NODE = 32
N_LOCAL = 8


def head_classes(key, slow_share):
    return jax.random.uniform(key, (VALUE_HEADS,)) < slow_share


def draw_log_decay(key, part):
    slow_share = 0.5
    slow_heads = head_classes(key, slow_share)
    key = jax.random.fold_in(key, 3)
    parallel_flows = jax.random.split(key, 6)
    slow_rate = jnp.exp(jax.random.uniform(parallel_flows[0], (VALUE_HEADS,), minval=jnp.log(0.15), maxval=jnp.log(0.45))) / SEQUENCE_TOKENS
    fast_rate = jnp.exp(jax.random.uniform(parallel_flows[1], (VALUE_HEADS,), minval=jnp.log(1.0 / 50.0), maxval=jnp.log(1.0 / 30.0)))
    baseline_rate = jnp.where(slow_heads, slow_rate, fast_rate)
    jaggedness = jax.random.uniform(parallel_flows[2], (SEQUENCE_TOKENS, VALUE_HEADS), minval=0.5, maxval=1.5)
    split_multiplier = jnp.exp(jax.random.uniform(parallel_flows[3], (SEQUENCE_TOKENS // TOK_NODE, 1, VALUE_HEADS), minval=jnp.log(0.5), maxval=jnp.log(2.0)))
    split_multiplier = jnp.broadcast_to(split_multiplier, (SEQUENCE_TOKENS // TOK_NODE, TOK_NODE, VALUE_HEADS)).reshape(SEQUENCE_TOKENS, VALUE_HEADS)
    spike_positions = jax.random.randint(parallel_flows[4], (3,), 0, SEQUENCE_TOKENS)
    spike_loss = -jnp.log(jax.random.uniform(parallel_flows[5], (3, VALUE_HEADS), minval=0.65, maxval=0.8))
    match_count = (jnp.arange(SEQUENCE_TOKENS)[:, None] == spike_positions[None, :]).astype(jnp.float32)
    spike_events = jnp.sum(match_count[:, :, None] * spike_loss[None, :, :], axis=1)
    return -(baseline_rate * jaggedness * split_multiplier + spike_events)


def draw_write_rate(key, part):
    slow_share = 0.5
    slow_heads = head_classes(key, slow_share)
    key = jax.random.fold_in(key, 5)
    parallel_flows = jax.random.split(key, 3)
    slow_level = jnp.exp(jax.random.uniform(parallel_flows[0], (VALUE_HEADS,), minval=jnp.log(4.0), maxval=jnp.log(12.0))) * DK / (64.0 * SEQUENCE_TOKENS)
    fast_level = jnp.exp(jax.random.uniform(parallel_flows[1], (VALUE_HEADS,), minval=jnp.log(0.3), maxval=jnp.log(0.9)))
    level = jnp.where(slow_heads, slow_level, fast_level)
    return level * jax.random.uniform(parallel_flows[2], (SEQUENCE_TOKENS, VALUE_HEADS), minval=0.5, maxval=1.1)


def level_of(stream_key, shape, cuts, low, largest):
    factor_of, own = 1.0, jax.random.fold_in(stream_key, 6)
    for dim, blocks in cuts:
        steps = jnp.exp(jax.random.uniform(jax.random.fold_in(own, dim), (blocks,), jnp.float32, low / len(cuts), largest / len(cuts)))
        factor_of = factor_of * jnp.repeat(steps, shape[dim] // blocks).reshape([-1 if axis == dim else 1 for axis in range(len(shape))])
    return factor_of


def shared_out(own_key, own, number, rows, number_of, top, reach, skew):
    ranking = jax.random.permutation(own_key, number_of)
    heavy_load, ordinary = load_shares(number_of, rows * top, reach, skew, True), load_shares(number_of, rows * top, reach, skew, False)
    places = jnp.arange(number_of)

    def named(lengths, offset_by):
        used = int((lengths > 0).sum())
        fixed = max(1, used // 4)
        passed = fixed + (places - fixed + offset_by * (used - fixed)) % max(1, number_of - fixed)
        return jnp.zeros((number_of,), jnp.int32).at[ranking[jnp.where(places < fixed, places, passed)]].set(jnp.asarray(lengths, jnp.int32))

    lengths = jnp.where(number % 4 == 0, named(heavy_load, number // 4), named(ordinary, number - number // 4 - 1))
    mixed = jax.random.permutation(jax.random.fold_in(own, 3), number_of)
    giver, receiver = mixed[0:number_of // 2 * 2:2], mixed[1:number_of // 2 * 2:2]
    slack = jnp.minimum(lengths[giver] - 1, reach - lengths[receiver]) // 2
    slack = jnp.where((giver == ranking[0]) | (receiver == ranking[0]) | (lengths[receiver] == 0), 0, jnp.maximum(slack, 0))
    passed = jax.random.randint(jax.random.fold_in(own, 4), (number_of // 2,), 0, 1 << 20) % (slack + 1)
    lengths = lengths.at[giver].add(-passed).at[receiver].add(passed)
    labels = jnp.searchsorted(jnp.cumsum(lengths), jnp.arange(rows * top), side="right").astype(jnp.int32)
    grid = labels.reshape(top, rows).T
    grid = grid[jax.random.permutation(jax.random.fold_in(own, 1), rows)]
    offset_by = jax.random.randint(jax.random.fold_in(own, 2), (rows, 1), 0, top)
    return jnp.take_along_axis(grid, (jnp.arange(top)[None, :] + offset_by) % top, axis=1)


def load_shares(amount, total, most, skew, full):
    weights = [(1 << 20) // math.isqrt(rank ** skew) + 1 for rank in range(1, amount + 1)]
    largest = most if full else min(most, max(-(-total // amount), total * weights[0] // sum(weights)))
    least = 1 if total - largest >= amount - 1 else 0
    holding, rest = [largest] + [least] * (amount - 1), total - largest - least * (amount - 1)
    while rest > 0:
        free = [i for i in range(1, amount) if holding[i] < largest] or [i for i in range(1, amount) if holding[i] < most]
        whole, left = sum([weights[i] for i in free]), rest
        for i in free:
            addition = min(most - holding[i], max(1, left * weights[i] // whole), rest)
            holding[i] = holding[i] + addition
            rest = rest - addition
    return np.array(holding)


def gaussian(rng, shape, scale, limit, cuts=(), kind=jnp.bfloat16):
    values = scale * jax.random.normal(rng, shape, jnp.float32)
    if cuts:
        values = values * level_of(rng, shape, cuts, -0.22, 0.18)
    return jnp.clip(values, -limit, limit).astype(kind)


def setup_inputs(seed: int = 0) -> dict:
    streams_of = jax.random.split(jax.random.key(seed), 15)
    hidden_in = gaussian(streams_of[0], (SEQUENCE_TOKENS, D), 1.0, 6.0, ((0, 256),))
    queries = gaussian(streams_of[1], (SEQUENCE_TOKENS, HK * DK), 1.0, 6.0, ((0, 32), (1, 8)))
    key_vectors = gaussian(streams_of[2], (SEQUENCE_TOKENS, HK * DK), 1.0, 6.0, ((0, 32), (1, 8)))
    values = gaussian(streams_of[3], (SEQUENCE_TOKENS, VALUE_HEADS * DV), 1.0, 6.0, ((0, 32), (1, 8)))
    out_gate = gaussian(streams_of[4], (SEQUENCE_TOKENS, VALUE_HEADS * DV), 1.0, 6.0, ((0, 32), (1, 8)))
    log_decay = draw_log_decay(jax.random.fold_in(streams_of[14], 71), 0)
    write_rate = draw_write_rate(jax.random.fold_in(streams_of[14], 71), 0)
    norm_gain = jnp.clip(1.0 + 0.1 * jax.random.normal(streams_of[7], (DV,), jnp.float32), 0.5, 1.5)
    out_weight = gaussian(streams_of[8], (VALUE_HEADS * DV, D), (VALUE_HEADS * DV) ** -0.5, 0.09375, ((0, 8),))
    post_gain = jnp.clip(1.0 + 0.1 * jax.random.normal(streams_of[9], (D,), jnp.float32), 0.5, 1.5)
    expert_index_keys = jax.random.split(jax.random.fold_in(streams_of[10], 1), SEQUENCE_TOKENS // TOK_NODE)
    expert_index_turns = jax.random.permutation(jax.random.fold_in(streams_of[10], 3), SEQUENCE_TOKENS // TOK_NODE)
    expert_index = jax.vmap(lambda own, number: shared_out(jax.random.fold_in(streams_of[10], 2), own, number, TOK_NODE, EXPERTS, TOP, CAP, 1))(expert_index_keys, expert_index_turns).reshape((SEQUENCE_TOKENS, TOP))
    route_weight = jnp.clip(jnp.exp(math.log(0.5) - 2.3025851 * jax.random.uniform(streams_of[11], (SEQUENCE_TOKENS, TOP), jnp.float32) ** level_of(streams_of[11], (SEQUENCE_TOKENS, TOP), ((0, 32),), -0.2, 0.2)), 0.05, 0.5)
    expert_gate_up = gaussian(streams_of[12], (EXPERTS, D, 2 * FFE), D ** -0.5, 0.125, ((0, 256),))
    expert_down = gaussian(streams_of[13], (EXPERTS, FFE, D), FFE ** -0.5, 0.25, ((0, 256),))
    return {"hidden_in": hidden_in, "queries": queries, "key_vectors": key_vectors, "values": values, "out_gate": out_gate, "log_decay": log_decay, "write_rate": write_rate, "norm_gain": norm_gain, "out_weight": out_weight, "post_gain": post_gain, "expert_index": expert_index, "route_weight": route_weight, "expert_gate_up": expert_gate_up, "expert_down": expert_down}


exact_precision = lax.Precision.HIGHEST

def unit_rows(matrix):
    return matrix * lax.rsqrt(lax.optimization_barrier(jnp.sum(matrix * matrix, axis=-1, keepdims=True)) + 1e-06)

def rms_normalize(matrix, gain_vector):
    return matrix * lax.rsqrt(lax.optimization_barrier(jnp.mean(matrix * matrix, axis=-1, keepdims=True)) + 1e-06) * gain_vector

def invert_unit_lower(lower_part):
    width_rows = lower_part.shape[-1]
    identity_matrix = jnp.eye(width_rows, dtype=jnp.float32)
    powered = -lower_part
    inverse = identity_matrix + powered
    for doubling in range(width_rows.bit_length() - 2):
        powered = jnp.einsum('...ij,...jk->...ik', powered, powered, precision=exact_precision)
        inverse = jnp.einsum('...ij,...jk->...ik', inverse, identity_matrix + powered, precision=exact_precision)
    return inverse

def block_terms(query_unit, key_unit, value_rows, cumulative, strength):
    width_rows = cumulative.shape[-1]
    positions = jnp.arange(width_rows)
    strict = positions[:, None] > positions[None, :]
    inclusive = positions[:, None] >= positions[None, :]
    spread = cumulative[..., :, None] - cumulative[..., None, :]
    decay_strict = jnp.where(strict, jnp.exp(jnp.where(strict, spread, 0.0)), 0.0)
    decay_inclusive = jnp.where(inclusive, jnp.exp(jnp.where(inclusive, spread, 0.0)), 0.0)
    key_inner = jnp.einsum('...td,...sd->...ts', key_unit, key_unit, precision=exact_precision)
    inverse = invert_unit_lower(strength[..., :, None] * decay_strict * key_inner)
    weight_values = jnp.einsum('...ts,...sv->...tv', inverse, strength[..., None] * value_rows, precision=exact_precision)
    weight_keys = jnp.einsum('...ts,...sk->...tk', inverse, (strength * jnp.exp(cumulative))[..., None] * key_unit, precision=exact_precision)
    attention = decay_inclusive * jnp.einsum('...td,...sd->...ts', query_unit, key_unit, precision=exact_precision)
    emitter = jnp.exp(cumulative)[..., None] * query_unit - jnp.einsum('...ts,...sk->...tk', attention, weight_keys, precision=exact_precision)
    tail_keys = jnp.exp(cumulative[..., -1:] - cumulative)[..., None] * key_unit
    identity_matrix = jnp.eye(key_unit.shape[-1], dtype=jnp.float32)
    transition = jnp.exp(cumulative[..., -1])[..., None, None] * identity_matrix - jnp.einsum('...tk,...tj->...kj', weight_keys, tail_keys, precision=exact_precision)
    injection = jnp.einsum('...tv,...tj->...vj', weight_values, tail_keys, precision=exact_precision)
    return (attention, weight_values, emitter, transition, injection)

def reference(hidden_in, queries, key_vectors, values, out_gate, log_decay, write_rate, norm_gain, out_weight, post_gain, expert_index, route_weight, expert_gate_up, expert_down):
    block_count = SEQUENCE_TOKENS // BLOCK
    inputs = (queries.reshape(block_count, BLOCK, HK * DK), key_vectors.reshape(block_count, BLOCK, HK * DK), values.reshape(block_count, BLOCK, VALUE_HEADS * DV), out_gate.reshape(block_count, BLOCK, VALUE_HEADS * DV), log_decay.reshape(block_count, BLOCK, VALUE_HEADS), write_rate.reshape(block_count, BLOCK, VALUE_HEADS))

    def advance(state_now, pieces):
        query_block, key_block, value_block, gate_block, decay_block, strength_block = pieces
        query_unit = unit_rows(query_block.astype(jnp.float32).reshape(BLOCK, HK, DK)) * DK ** (-0.5)
        query_unit = jnp.swapaxes(jnp.repeat(query_unit, VALUE_HEADS // HK, axis=1), 0, 1)
        key_unit = jnp.swapaxes(jnp.repeat(unit_rows(key_block.astype(jnp.float32).reshape(BLOCK, HK, DK)), VALUE_HEADS // HK, axis=1), 0, 1)
        value_rows = jnp.swapaxes(value_block.astype(jnp.float32).reshape(BLOCK, VALUE_HEADS, DV), 0, 1)
        cumulative = jnp.cumsum(decay_block, axis=0).T
        attention, weight_values, emitter, transition, injection = block_terms(query_unit, key_unit, value_rows, cumulative, strength_block.T)
        core_out = jnp.einsum('htk,hvk->htv', emitter, state_now, precision=exact_precision)
        core_out = core_out + jnp.einsum('hts,hsv->htv', attention, weight_values, precision=exact_precision)
        state_next = jnp.einsum('hvk,hkj->hvj', state_now, transition, precision=exact_precision) + injection
        core_out = jnp.swapaxes(core_out, 0, 1)
        gate_rows = gate_block.astype(jnp.float32).reshape(BLOCK, VALUE_HEADS, DV)
        gated = rms_normalize(core_out, norm_gain) * jax.nn.silu(gate_rows)
        return (state_next, gated.reshape(BLOCK, VALUE_HEADS * DV).astype(jnp.bfloat16))
    initial = jnp.zeros((VALUE_HEADS, DV, DK), jnp.float32)
    final_state, gated = lax.scan(advance, initial, inputs)
    gated = gated.reshape(SEQUENCE_TOKENS, VALUE_HEADS * DV)
    columns = HV_DEV * DV
    hidden_state = hidden_in.astype(jnp.float32)
    for group_index in range(N_LOCAL):
        partial_value = jnp.dot(gated[:, group_index * columns:(group_index + 1) * columns], out_weight[group_index * columns:(group_index + 1) * columns], preferred_element_type=jnp.float32)
        hidden_state = hidden_state + lax.optimization_barrier(partial_value.astype(jnp.bfloat16)).astype(jnp.float32)
    normed = rms_normalize(hidden_state, post_gain).astype(jnp.bfloat16)
    pair_total = SEQUENCE_TOKENS * TOP
    flat_index = expert_index.reshape(-1)
    flat_weight = jnp.concatenate([route_weight.reshape(-1), jnp.zeros((1,), jnp.float32)])
    padded_rows = jnp.concatenate([normed, jnp.zeros((1, D), jnp.bfloat16)], axis=0)
    limit_rows = N_NODE * CAP

    def expert_apply(accumulated, expert):
        chosen = jnp.nonzero(flat_index == expert, size=limit_rows, fill_value=pair_total)[0].astype(jnp.int32)
        tokens = chosen // TOP
        weights = flat_weight[chosen]
        gate_up = jnp.dot(padded_rows[tokens], expert_gate_up[expert], preferred_element_type=jnp.float32)
        hidden_rows = (jax.nn.silu(gate_up[:, :FFE]) * gate_up[:, FFE:]).astype(jnp.bfloat16)
        output_rows = jnp.dot(hidden_rows, expert_down[expert], preferred_element_type=jnp.float32).astype(jnp.bfloat16)
        accumulated = accumulated.at[tokens].add(weights[:, None] * output_rows.astype(jnp.float32), mode='drop')
        return (accumulated, None)
    running = hidden_state
    for group_index in range(N_LOCAL):
        members = ((jnp.arange(N_NODE)[:, None] * N_LOCAL + group_index) * EXP_DEV + jnp.arange(EXP_DEV)[None, :]).reshape(-1).astype(jnp.int32)
        accumulated, unused = lax.scan(expert_apply, jnp.zeros((SEQUENCE_TOKENS, D), jnp.float32), members)
        running = running + lax.optimization_barrier(accumulated.astype(jnp.bfloat16)).astype(jnp.float32)
    return running.astype(jnp.bfloat16)
```

```python
import jax
import jax.numpy as jnp
from jax import lax
from jax.experimental import pallas as pl
from jax.experimental.pallas import tpu as pltpu
from jax.sharding import PartitionSpec as P

DK = 128
DV = 128
HEADS = 4
BLOCK = 64
STACK = HEADS * BLOCK
SPLIT = 8
LOCAL = 8

f32 = jnp.float32
bf16 = jnp.bfloat16


def mm(a, b):
    return jnp.dot(a.astype(bf16), b.astype(bf16), preferred_element_type=f32)


def mm_t(a, b):
    return lax.dot_general(
        a.astype(bf16), b.astype(bf16), (((1,), (1,)), ((), ())), preferred_element_type=f32
    )


def t_mm(a, b):
    return lax.dot_general(
        a.astype(bf16), b.astype(bf16), (((0,), (0,)), ((), ())), preferred_element_type=f32
    )


def stack_rows(pieces):
    return jnp.concatenate(pieces, axis=0)


def head_column(columns):
    return stack_rows([columns[:, h : h + 1] for h in range(HEADS)])


def unit_scale(rows):
    wide = rows.astype(f32)
    return lax.rsqrt(jnp.sum(wide * wide, axis=-1, keepdims=True) + 1e-06)


def stacked_keys(key_ref, rows):
    keys = key_ref[rows, :]
    pair = [keys[:, :DK], keys[:, DK:]]
    scales = [unit_scale(p) for p in pair]
    return (
        stack_rows([pair[0], pair[0], pair[1], pair[1]]),
        stack_rows([scales[0], scales[0], scales[1], scales[1]]),
    )


def grid_places():
    row = lax.broadcasted_iota(jnp.int32, (STACK, STACK), 0)
    col = lax.broadcasted_iota(jnp.int32, (STACK, STACK), 1)
    return row, col, (row // BLOCK) == (col // BLOCK)


def as_row(column, row, col):
    return jnp.sum(jnp.where(row == col, column, 0.0), axis=0, keepdims=True)


def maps_kernel(
    key_ref, value_ref, decay_ref, rate_ref,
    payload_ref, cum_ref, inner_ref, values_ref, starts_ref,
    rate_s, tail_s, state_s,
):
    tokens = key_ref.shape[0]
    blocks = tokens // BLOCK
    lane = lax.broadcasted_iota(jnp.int32, (HEADS, tokens), 1) % BLOCK
    total = decay_ref[...]
    step = 1
    while step < BLOCK:
        total = total + jnp.where(lane >= step, pltpu.roll(total, step, 1), 0.0)
        step *= 2
    cum_ref[...] = total.T
    rate_s[...] = rate_ref[...].T

    def one_block(b):
        rows = pl.ds(b * BLOCK, BLOCK)
        row, col, same = grid_places()
        keys, scale = stacked_keys(key_ref, rows)
        cum = cum_ref[rows, :]
        cum_col = head_column(cum)
        rate_col = head_column(rate_s[rows, :])
        last_col = stack_rows(
            [jnp.broadcast_to(cum[BLOCK - 1 : BLOCK, h : h + 1], (BLOCK, 1)) for h in range(HEADS)]
        )
        strict = jnp.logical_and(same, row > col)
        spread = jnp.where(strict, cum_col - as_row(cum_col, row, col), 0.0)
        power = jnp.where(
            strict,
            -(jnp.exp(spread) * mm_t(keys, keys)) * ((rate_col * scale) * as_row(scale, row, col)),
            0.0,
        )
        raw = value_ref[rows, :]
        wide = keys.astype(f32)
        answer = jnp.concatenate(
            [
                rate_col * stack_rows([raw[:, h * DV : (h + 1) * DV] for h in range(HEADS)]).astype(f32),
                (rate_col * jnp.exp(cum_col) * scale) * wide,
            ],
            axis=1,
        )
        reach = 1
        while reach < BLOCK:
            answer = answer + mm(power, answer)
            reach *= 2
            if reach < BLOCK:
                power = mm(power, power)
        values_ref[b] = answer[:, :DV]
        inner_ref[b] = answer[:, DV:].astype(bf16)
        tail_s[b] = ((jnp.exp(last_col - cum_col) * scale) * wide).astype(bf16)

    def two_blocks(i, carry):
        one_block(2 * i)
        one_block(2 * i + 1)
        return carry

    lax.fori_loop(0, blocks // 2, two_blocks, 0)

    place = lax.broadcasted_iota(jnp.int32, (DK, DV + DK), 0)
    lane_place = lax.broadcasted_iota(jnp.int32, (DK, DV + DK), 1)
    for h in range(HEADS):
        state_s[h] = jnp.where(lane_place == place + DV, 1.0, 0.0)

    def advance(b, carry):
        last = cum_ref[pl.ds(b * BLOCK + BLOCK - 1, 1), :]
        for h in range(HEADS):
            part = slice(h * BLOCK, (h + 1) * BLOCK)
            state = state_s[h]
            rounded = state.astype(bf16)
            starts_ref[b, h] = rounded
            change = mm(inner_ref[b, part, :], rounded)
            given = jnp.concatenate([values_ref[b, part, :] - change[:, :DV], -change[:, DV:]], axis=1)
            state_s[h] = jnp.exp(last[:, h : h + 1]) * state + t_mm(tail_s[b, part, :], given)
        return carry

    lax.fori_loop(0, blocks, advance, 0)
    share = DV // SPLIT
    for h in range(HEADS):
        state = state_s[h]
        inject = state[:, :DV].T.astype(bf16)
        move = state[:, DV:].T.astype(bf16)
        for s in range(SPLIT):
            payload_ref[h * SPLIT + s, :DK, :] = move
            payload_ref[h * SPLIT + s, DK:, :] = inject[s * share : (s + 1) * share, :]


def shard_maps(keys, values, decay, rate):
    tokens = keys.shape[0]
    blocks = tokens // BLOCK
    return pl.pallas_call(
        maps_kernel,
        out_shape=(
            jax.ShapeDtypeStruct((HEADS * SPLIT, DK + DV // SPLIT, DK), bf16),
            jax.ShapeDtypeStruct((tokens, HEADS), f32),
            jax.ShapeDtypeStruct((blocks, STACK, DK), bf16),
            jax.ShapeDtypeStruct((blocks, STACK, DV), f32),
            jax.ShapeDtypeStruct((blocks, HEADS, DK, DV + DK), bf16),
        ),
        scratch_shapes=[
            pltpu.VMEM((tokens, HEADS), f32),
            pltpu.VMEM((blocks, STACK, DK), bf16),
            pltpu.VMEM((HEADS, DK, DV + DK), f32),
        ],
        compiler_params=pltpu.CompilerParams(vmem_limit_bytes=48 * 2**20),
        name="shard_maps",
    )(keys, values, decay, rate)


def reads_kernel(query_ref, key_ref, cum_ref, inner_ref, values_ref, starts_ref, core_ref, reach_ref):
    blocks = query_ref.shape[0] // BLOCK

    def one_block(b):
        rows = pl.ds(b * BLOCK, BLOCK)
        row, col, same = grid_places()
        keys, scale = stacked_keys(key_ref, rows)
        queries, query_scale = stacked_keys(query_ref, rows)
        query_scale = query_scale * DK ** (-0.5)
        cum_col = head_column(cum_ref[rows, :])
        inclusive = jnp.logical_and(same, row >= col)
        spread = jnp.where(inclusive, cum_col - as_row(cum_col, row, col), 0.0)
        attention = jnp.where(
            inclusive,
            jnp.exp(spread) * mm_t(queries, keys) * (query_scale * as_row(scale, row, col)),
            0.0,
        )
        both = mm(attention, jnp.concatenate([values_ref[b].astype(bf16), inner_ref[b]], axis=1))
        emitter = ((jnp.exp(cum_col) * query_scale) * queries.astype(f32) - both[:, DV:]).astype(bf16)
        for h in range(HEADS):
            part = slice(h * BLOCK, (h + 1) * BLOCK)
            read = mm(emitter[part, :], starts_ref[b, h])
            core_ref[rows, h * DV : (h + 1) * DV] = both[part, :DV] + read[:, :DV]
            reach_ref[rows, h * DK : (h + 1) * DK] = read[:, DV:].astype(bf16)

    def two_blocks(i, carry):
        one_block(2 * i)
        one_block(2 * i + 1)
        return carry

    lax.fori_loop(0, blocks // 2, two_blocks, 0)


def block_reads(queries, keys, cum, inner, values, starts):
    tokens = keys.shape[0]
    return pl.pallas_call(
        reads_kernel,
        out_shape=(
            jax.ShapeDtypeStruct((tokens, HEADS * DV), f32),
            jax.ShapeDtypeStruct((tokens, HEADS * DK), bf16),
        ),
        compiler_params=pltpu.CompilerParams(vmem_limit_bytes=48 * 2**20),
        cost_estimate=pl.CostEstimate(flops=2 * 10**9, bytes_accessed=8 * 10**6, transcendentals=10**6),
        name="block_reads",
    )(queries, keys, cum, inner, values, starts)


def chain_kernel(maps_ref, start_ref):
    share = start_ref.shape[1]
    state = jnp.zeros((share, DK), f32)
    for k in range(maps_ref.shape[0]):
        high = state.astype(bf16)
        start_ref[k] = high
        low = (state - high.astype(f32)).astype(bf16)
        moved = jnp.dot(
            jnp.concatenate([high, low], axis=0), maps_ref[k, :DK, :], preferred_element_type=f32
        )
        state = moved[:share] + moved[share:] + maps_ref[k, DK:, :].astype(f32)


def chain(maps):
    return pl.pallas_call(
        chain_kernel,
        out_shape=jax.ShapeDtypeStruct((maps.shape[0], maps.shape[1] - DK, DK), bf16),
        compiler_params=pltpu.CompilerParams(vmem_limit_bytes=32 * 2**20),
        name="state_chain",
    )(maps)


def gated_kernel(core_side, core_ref, reach_ref, start_ref, gate_ref, gain_ref, own_ref, other_ref):
    tokens = core_ref.shape[0]
    share = tokens // LOCAL
    side = core_side[0]
    for chip in range(LOCAL // 2):
        for ref, parity in ((own_ref, side), (other_ref, 1 - side)):
            rows = pl.ds((2 * chip + parity) * share, share)
            for h in range(HEADS):
                lanes = slice(h * DV, (h + 1) * DV)
                core = core_ref[rows, lanes] + mm_t(reach_ref[rows, lanes], start_ref[lanes, :])
                core = core * lax.rsqrt(jnp.mean(core * core, axis=-1, keepdims=True) + 1e-06)
                gate = gate_ref[rows, lanes].astype(f32)
                ref[chip * share : (chip + 1) * share, lanes] = (
                    core * gain_ref[...] * (gate / (1.0 + jnp.exp(-gate)))
                ).astype(bf16)


def gated_halves(side, core, reach, starts, gate, gain):
    tokens = core.shape[0]
    vmem = pl.BlockSpec(memory_space=pltpu.VMEM)
    half = jax.ShapeDtypeStruct((tokens // 2, HEADS * DV), bf16)
    return pl.pallas_call(
        gated_kernel,
        out_shape=(half, half),
        in_specs=[pl.BlockSpec(memory_space=pltpu.SMEM)] + [vmem] * 5,
        out_specs=(vmem, vmem),
        compiler_params=pltpu.CompilerParams(vmem_limit_bytes=32 * 2**20),
        name="gated_halves",
    )(side, core, reach, starts, gate, gain)


def project_kernel(own_ref, other_ref, own_weight, other_weight, out_ref):
    out_ref[...] = (mm(own_ref[...], own_weight[...]) + mm(other_ref[...], other_weight[...])).astype(bf16)


def project(own, other, own_weight, other_weight):
    rows, depth = own.shape
    width = own_weight.shape[1]
    tile = 512
    rows_spec = pl.BlockSpec((rows, depth), lambda i: (0, 0))
    weight_spec = pl.BlockSpec((depth, tile), lambda i: (0, i))
    return pl.pallas_call(
        project_kernel,
        out_shape=jax.ShapeDtypeStruct((rows, width), bf16),
        grid=(width // tile,),
        in_specs=[rows_spec, rows_spec, weight_spec, weight_spec],
        out_specs=pl.BlockSpec((rows, tile), lambda i: (0, i)),
        compiler_params=pltpu.CompilerParams(vmem_limit_bytes=32 * 2**20),
        name="project",
    )(own, other, own_weight, other_weight)


def residual_kernel(parts_ref, hidden_ref, gain_ref, state_ref, normed_ref):
    state = hidden_ref[...].astype(f32)
    for part in range(parts_ref.shape[0]):
        state = state + parts_ref[part].astype(f32)
    state_ref[...] = state
    normed = state * lax.rsqrt(jnp.mean(state * state, axis=-1, keepdims=True) + 1e-06) * gain_ref[...]
    for copy in range(normed_ref.shape[0]):
        normed_ref[copy] = normed.astype(bf16)


def residual(parts, hidden, gain):
    return pl.pallas_call(
        residual_kernel,
        out_shape=(
            jax.ShapeDtypeStruct(hidden.shape, f32),
            jax.ShapeDtypeStruct(parts.shape, bf16),
        ),
        compiler_params=pltpu.CompilerParams(vmem_limit_bytes=32 * 2**20),
        name="residual",
    )(parts, hidden, gain)


def routing_kernel(capacity, place_ref, index_ref, weight_ref, pick_ref, merge_ref, slot_s, share_s, wide_s):
    top, tokens = index_ref.shape
    groups = slot_s.shape[0]
    ids = lax.broadcasted_iota(jnp.int32, (groups, 1), 0) * LOCAL + place_ref[0]
    member = jnp.zeros((groups, tokens), f32)
    share = jnp.zeros((groups, tokens), f32)
    for j in range(top):
        hit = index_ref[j : j + 1, :] == ids
        member = jnp.where(hit, 1.0, member)
        share = jnp.where(hit, weight_ref[j : j + 1, :], share)
    earlier = lax.broadcasted_iota(jnp.int32, (tokens, tokens), 0) < lax.broadcasted_iota(
        jnp.int32, (tokens, tokens), 1
    )
    rank = mm(member, jnp.where(earlier, 1.0, 0.0))
    slot_s[...] = jnp.where(member > 0.0, rank, -1.0)
    share_s[...] = share
    several = 4
    span = several * capacity
    for i in range(groups // several):
        slot = slot_s[i * several : (i + 1) * several, :]
        part = share_s[i * several : (i + 1) * several, :]
        place = lax.broadcasted_iota(jnp.int32, (several, capacity, tokens), 1).astype(f32)
        hit = slot[:, None, :] == place
        pick_ref[i * span : (i + 1) * span, :] = (
            jnp.where(hit, 1.0, 0.0).reshape(span, tokens).astype(bf16)
        )
        wide_s[i * span : (i + 1) * span, :] = jnp.where(hit, part[:, None, :], 0.0).reshape(
            span, tokens
        )
    for i in range(groups * capacity // 128):
        merge_ref[:, i * 128 : (i + 1) * 128] = wide_s[i * 128 : (i + 1) * 128, :].T.astype(bf16)


def routing(place, index, weight, groups, capacity):
    top, tokens = index.shape
    slots = groups * capacity
    vmem = pl.BlockSpec(memory_space=pltpu.VMEM)
    return pl.pallas_call(
        lambda *refs: routing_kernel(capacity, *refs),
        out_shape=(
            jax.ShapeDtypeStruct((slots, tokens), bf16),
            jax.ShapeDtypeStruct((tokens, slots), bf16),
        ),
        in_specs=[pl.BlockSpec(memory_space=pltpu.SMEM), vmem, vmem],
        out_specs=(vmem, vmem),
        scratch_shapes=[
            pltpu.VMEM((groups, tokens), f32),
            pltpu.VMEM((groups, tokens), f32),
            pltpu.VMEM((slots, tokens), f32),
        ],
        compiler_params=pltpu.CompilerParams(vmem_limit_bytes=32 * 2**20),
        cost_estimate=pl.CostEstimate(flops=3 * 10**9, bytes_accessed=6 * 10**6, transcendentals=0),
        name="routing",
    )(place, index, weight)


def pick_kernel(pick_ref, own_ref, other_ref, out_ref):
    half = own_ref.shape[0]
    out_ref[...] = (mm(pick_ref[:, :half], own_ref[...]) + mm(pick_ref[:, half:], other_ref[...])).astype(bf16)


def pick_rows(pick, own, other):
    slots, tokens = pick.shape
    half, width = own.shape
    tile = 512
    half_spec = pl.BlockSpec((half, tile), lambda i: (0, i))
    return pl.pallas_call(
        pick_kernel,
        out_shape=jax.ShapeDtypeStruct((slots, width), bf16),
        grid=(width // tile,),
        in_specs=[pl.BlockSpec((slots, tokens), lambda i: (0, 0)), half_spec, half_spec],
        out_specs=pl.BlockSpec((slots, tile), lambda i: (0, i)),
        compiler_params=pltpu.CompilerParams(vmem_limit_bytes=32 * 2**20),
        name="pick_rows",
    )(pick, own, other)


def merge_kernel(merge_ref, rows_ref, out_ref):
    out_ref[...] = mm(merge_ref[...], rows_ref[...]).astype(bf16)


def merge_add_kernel(merge_ref, rows_ref, add_ref, out_ref):
    out_ref[...] = (mm(merge_ref[...], rows_ref[...]) + add_ref[...].astype(f32)).astype(bf16)


def merge_rows(merge, half, rows, *add):
    tokens, slots = merge.shape
    width = rows.shape[1]
    tile = 512
    out_spec = pl.BlockSpec((tokens // 2, tile), lambda i: (0, i))
    return pl.pallas_call(
        merge_add_kernel if add else merge_kernel,
        out_shape=jax.ShapeDtypeStruct((tokens // 2, width), bf16),
        grid=(width // tile,),
        in_specs=[
            pl.BlockSpec((tokens // 2, slots), lambda i: (half, 0)),
            pl.BlockSpec((slots, tile), lambda i: (0, i)),
        ]
        + [out_spec] * len(add),
        out_specs=out_spec,
        compiler_params=pltpu.CompilerParams(vmem_limit_bytes=32 * 2**20),
        name="merge_rows",
    )(merge, rows, *add)


def swap_cores(array):
    return lax.ppermute(array, "local", [(i, i ^ 1) for i in range(LOCAL)])


def across_chips(array):
    groups = [[side + 2 * chip for chip in range(LOCAL // 2)] for side in range(2)]
    return lax.all_to_all(
        array, "local", split_axis=0, concat_axis=0, tiled=True, axis_index_groups=groups
    )


def across_nodes(array):
    return lax.all_to_all(array, "node", split_axis=0, concat_axis=0, tiled=True)


def local(
    hidden_in, queries, key_vectors, values, out_gate, log_decay, write_rate, norm_gain,
    out_weight, post_gain, expert_index, route_weight, expert_gate_up, expert_down,
):
    node_count = lax.axis_size("node")
    local_index = lax.axis_index("local")
    side = local_index % 2
    tokens, top = expert_index.shape
    chips = LOCAL // 2
    share = tokens // LOCAL
    width = hidden_in.shape[1]
    capacity = 6 * tokens * top // (5 * node_count * LOCAL)
    side_array = side.astype(jnp.int32).reshape(1)

    other_weight = swap_cores(out_weight)

    def by_side(array):
        split = array.T.reshape(top, chips, 2, share)
        split = jnp.where(side == 0, split, split[:, :, ::-1])
        return split.transpose(0, 2, 1, 3).reshape(top, tokens)

    pick, merge = routing(
        local_index.astype(jnp.int32).reshape(1), by_side(expert_index), by_side(route_weight),
        node_count, capacity,
    )

    payload, cum, inner, value_rows, starts = shard_maps(key_vectors, values, log_decay.T, write_rate.T)
    maps = across_nodes(payload)
    core, reach = block_reads(queries, key_vectors, cum, inner, value_rows, starts)
    carried = across_nodes(chain(maps)).reshape(HEADS * DV, DK)
    own_half, other_half = gated_halves(
        side_array, core, reach, carried, out_gate, norm_gain.reshape(1, DV)
    )
    partial = project(own_half, swap_cores(other_half), out_weight, other_weight)
    parts = across_chips(partial.reshape(chips, share, width))
    hidden_state, normed = residual(parts, hidden_in, post_gain.reshape(1, width))
    own_rows = across_chips(normed).reshape(chips * share, width)
    rows = pick_rows(pick, own_rows, swap_cores(own_rows)).reshape(node_count, capacity, width)
    rows = across_nodes(rows).reshape(node_count * capacity, width)
    gate_up = jnp.dot(rows, expert_gate_up[0], preferred_element_type=f32)
    half_width = gate_up.shape[1] // 2
    hidden_rows = (jax.nn.silu(gate_up[:, :half_width]) * gate_up[:, half_width:]).astype(bf16)
    results = jnp.dot(hidden_rows, expert_down[0], preferred_element_type=f32).astype(bf16)
    returned = across_nodes(results.reshape(node_count, capacity, width)).reshape(
        node_count * capacity, width
    )
    given = swap_cores(merge_rows(merge, 1, returned))
    summed = merge_rows(merge, 0, returned, given)
    arrived = across_chips(summed.reshape(chips, share, width))
    return (hidden_state + jnp.sum(arrived.astype(f32), axis=0)).astype(bf16)


def solution(mesh):
    return jax.shard_map(
        local,
        mesh=mesh,
        in_specs=(
            P(("node", "local"), None),
            P("node", "local"),
            P("node", "local"),
            P("node", "local"),
            P("node", "local"),
            P("node", "local"),
            P("node", "local"),
            P(),
            P("local", None),
            P(),
            P("node", None),
            P("node", None),
            P(("node", "local"), None, None),
            P(("node", "local"), None, None),
        ),
        out_specs=P(("node", "local"), None),
        check_vma=False,
    )
```

```python
import jax
import jax.numpy as jnp
from jax import lax
from jax.experimental import pallas as pl
from jax.experimental.pallas import tpu as pltpu
from jax.sharding import PartitionSpec as P

DK = 128
DV = 128
HEADS = 4
BLOCK = 64
STACK = HEADS * BLOCK
SPLIT = 2
NODE_ROW = 8
LOCAL = 8

f32 = jnp.float32
bf16 = jnp.bfloat16


def mm(a, b):
    return jnp.dot(a.astype(bf16), b.astype(bf16), preferred_element_type=f32)


def mm_t(a, b):
    return lax.dot_general(
        a.astype(bf16), b.astype(bf16), (((1,), (1,)), ((), ())), preferred_element_type=f32
    )


def t_mm(a, b):
    return lax.dot_general(
        a.astype(bf16), b.astype(bf16), (((0,), (0,)), ((), ())), preferred_element_type=f32
    )


def stack_rows(pieces):
    return jnp.concatenate(pieces, axis=0)


def head_column(columns):
    return stack_rows([columns[:, h : h + 1] for h in range(HEADS)])


def unit_scale(rows):
    wide = rows.astype(f32)
    return lax.rsqrt(jnp.sum(wide * wide, axis=-1, keepdims=True) + 1e-06)


def stacked_keys(key_ref, rows):
    keys = key_ref[rows, :]
    pair = [keys[:, :DK], keys[:, DK:]]
    scales = [unit_scale(p) for p in pair]
    return (
        stack_rows([pair[0], pair[0], pair[1], pair[1]]),
        stack_rows([scales[0], scales[0], scales[1], scales[1]]),
    )


def grid_places():
    row = lax.broadcasted_iota(jnp.int32, (STACK, STACK), 0)
    col = lax.broadcasted_iota(jnp.int32, (STACK, STACK), 1)
    return row, col, (row // BLOCK) == (col // BLOCK)


def as_row(column, row, col):
    return jnp.sum(jnp.where(row == col, column, 0.0), axis=0, keepdims=True)


def maps_kernel(
    key_ref, value_ref, decay_ref, rate_ref,
    payload_ref, cum_ref, inner_ref, values_ref, starts_ref,
    rate_s, tail_s, state_s, values_s,
):
    tokens = key_ref.shape[0]
    blocks = tokens // BLOCK
    lane = lax.broadcasted_iota(jnp.int32, (HEADS, tokens), 1) % BLOCK
    total = decay_ref[...]
    step = 1
    while step < BLOCK:
        total = total + jnp.where(lane >= step, pltpu.roll(total, step, 1), 0.0)
        step *= 2
    cum_ref[...] = total.T
    rate_s[...] = rate_ref[...].T

    def one_block(b):
        rows = pl.ds(b * BLOCK, BLOCK)
        row, col, same = grid_places()
        keys, scale = stacked_keys(key_ref, rows)
        cum = cum_ref[rows, :]
        cum_col = head_column(cum)
        rate_col = head_column(rate_s[rows, :])
        last_col = stack_rows(
            [jnp.broadcast_to(cum[BLOCK - 1 : BLOCK, h : h + 1], (BLOCK, 1)) for h in range(HEADS)]
        )
        strict = jnp.logical_and(same, row > col)
        spread = jnp.where(strict, cum_col - as_row(cum_col, row, col), 0.0)
        power = jnp.where(
            strict,
            -(jnp.exp(spread) * mm_t(keys, keys)) * ((rate_col * scale) * as_row(scale, row, col)),
            0.0,
        )
        raw = value_ref[rows, :]
        wide = keys.astype(f32)
        answer = jnp.concatenate(
            [
                rate_col * stack_rows([raw[:, h * DV : (h + 1) * DV] for h in range(HEADS)]).astype(f32),
                (rate_col * jnp.exp(cum_col) * scale) * wide,
            ],
            axis=1,
        )
        reach = 1
        while reach < BLOCK:
            answer = answer + mm(power, answer)
            reach *= 2
            if reach < BLOCK:
                power = mm(power, power)
        values_s[b] = answer[:, :DV]
        values_ref[b] = answer[:, :DV].astype(bf16)
        inner_ref[b] = answer[:, DV:].astype(bf16)
        tail_s[b] = ((jnp.exp(last_col - cum_col) * scale) * wide).astype(bf16)

    for b in range(blocks):
        one_block(b)

    place = lax.broadcasted_iota(jnp.int32, (DK, DV + DK), 0)
    lane_place = lax.broadcasted_iota(jnp.int32, (DK, DV + DK), 1)
    for h in range(HEADS):
        state_s[h] = jnp.where(lane_place == place + DV, 1.0, 0.0)

    def advance(b, carry):
        last = cum_ref[pl.ds(b * BLOCK + BLOCK - 1, 1), :]
        for h in range(HEADS):
            part = slice(h * BLOCK, (h + 1) * BLOCK)
            state = state_s[h]
            rounded = state.astype(bf16)
            starts_ref[b, h] = rounded
            change = mm(inner_ref[b, part, :], rounded)
            given = jnp.concatenate([values_s[b, part, :] - change[:, :DV], -change[:, DV:]], axis=1)
            state_s[h] = jnp.exp(last[:, h : h + 1]) * state + t_mm(tail_s[b, part, :], given)
        return carry

    lax.fori_loop(0, blocks, advance, 0, unroll=True)
    share = DV // SPLIT
    for h in range(HEADS):
        state = state_s[h]
        inject = state[:, :DV].T.astype(bf16)
        move = state[:, DV:].T.astype(bf16)
        for s in range(SPLIT):
            payload_ref[h * SPLIT + s, :DK, :] = move
            payload_ref[h * SPLIT + s, DK:, :] = inject[s * share : (s + 1) * share, :]


def shard_maps(keys, values, decay, rate):
    tokens = keys.shape[0]
    blocks = tokens // BLOCK
    return pl.pallas_call(
        maps_kernel,
        out_shape=(
            jax.ShapeDtypeStruct((HEADS * SPLIT, DK + DV // SPLIT, DK), bf16),
            jax.ShapeDtypeStruct((tokens, HEADS), f32),
            jax.ShapeDtypeStruct((blocks, STACK, DK), bf16),
            jax.ShapeDtypeStruct((blocks, STACK, DV), bf16),
            jax.ShapeDtypeStruct((blocks, HEADS, DK, DV + DK), bf16),
        ),
        scratch_shapes=[
            pltpu.VMEM((tokens, HEADS), f32),
            pltpu.VMEM((blocks, STACK, DK), bf16),
            pltpu.VMEM((HEADS, DK, DV + DK), f32),
            pltpu.VMEM((blocks, STACK, DV), f32),
        ],
        compiler_params=pltpu.CompilerParams(vmem_limit_bytes=60 * 2**20),
        name="shard_maps",
    )(keys, values, decay, rate)


def reads_kernel(query_ref, key_ref, cum_ref, inner_ref, values_ref, starts_ref, core_ref, reach_ref):
    blocks = query_ref.shape[0] // BLOCK

    def one_block(b):
        rows = pl.ds(b * BLOCK, BLOCK)
        row, col, same = grid_places()
        keys, scale = stacked_keys(key_ref, rows)
        queries, query_scale = stacked_keys(query_ref, rows)
        query_scale = query_scale * DK ** (-0.5)
        cum_col = head_column(cum_ref[rows, :])
        inclusive = jnp.logical_and(same, row >= col)
        spread = jnp.where(inclusive, cum_col - as_row(cum_col, row, col), 0.0)
        attention = jnp.where(
            inclusive,
            jnp.exp(spread) * mm_t(queries, keys) * (query_scale * as_row(scale, row, col)),
            0.0,
        )
        both = mm(attention, jnp.concatenate([values_ref[b], inner_ref[b]], axis=1))
        emitter = ((jnp.exp(cum_col) * query_scale) * queries.astype(f32) - both[:, DV:]).astype(bf16)
        for h in range(HEADS):
            part = slice(h * BLOCK, (h + 1) * BLOCK)
            read = mm(emitter[part, :], starts_ref[b, h])
            core_ref[rows, h * DV : (h + 1) * DV] = both[part, :DV] + read[:, :DV]
            reach_ref[rows, h * DK : (h + 1) * DK] = read[:, DV:].astype(bf16)

    for b in range(blocks):
        one_block(b)


def block_reads(queries, keys, cum, inner, values, starts):
    tokens = keys.shape[0]
    return pl.pallas_call(
        reads_kernel,
        out_shape=(
            jax.ShapeDtypeStruct((tokens, HEADS * DV), f32),
            jax.ShapeDtypeStruct((tokens, HEADS * DK), bf16),
        ),
        compiler_params=pltpu.CompilerParams(vmem_limit_bytes=60 * 2**20),
        cost_estimate=pl.CostEstimate(flops=2 * 10**9, bytes_accessed=8 * 10**6, transcendentals=10**6),
        name="block_reads",
    )(queries, keys, cum, inner, values, starts)


def step(state, move):
    rows = state.shape[0]
    high = state.astype(bf16)
    low = (state - high.astype(f32)).astype(bf16)
    moved = jnp.dot(jnp.concatenate([high, low], axis=0), move, preferred_element_type=f32)
    return moved[:rows] + moved[rows:]


def row_total_kernel(maps_ref, total_ref):
    total = maps_ref[0].astype(f32)
    for k in range(1, maps_ref.shape[0]):
        moved = step(total, maps_ref[k, :DK, :])
        total = jnp.concatenate([moved[:DK], moved[DK:] + maps_ref[k, DK:, :].astype(f32)], axis=0)
    for copy in range(total_ref.shape[0]):
        total_ref[copy] = total.astype(bf16)


def row_total(maps, rows):
    return pl.pallas_call(
        row_total_kernel,
        out_shape=jax.ShapeDtypeStruct((rows,) + maps.shape[1:], bf16),
        compiler_params=pltpu.CompilerParams(vmem_limit_bytes=32 * 2**20),
        name="row_total",
    )(maps)


def starts_kernel(row_ref, totals_ref, maps_ref, start_ref):
    def apply(state, ref, k):
        return step(state, ref[k, :DK, :]) + ref[k, DK:, :].astype(f32)

    state = jnp.zeros(start_ref.shape[1:], f32)
    for k in range(totals_ref.shape[0] - 1):
        state = jnp.where(k < row_ref[0], apply(state, totals_ref, k), state)
    for k in range(maps_ref.shape[0]):
        start_ref[k] = state.astype(bf16)
        if k + 1 < maps_ref.shape[0]:
            state = apply(state, maps_ref, k)


def shard_starts(row, totals, maps):
    vmem = pl.BlockSpec(memory_space=pltpu.VMEM)
    return pl.pallas_call(
        starts_kernel,
        out_shape=jax.ShapeDtypeStruct((maps.shape[0], maps.shape[1] - DK, DK), bf16),
        in_specs=[pl.BlockSpec(memory_space=pltpu.SMEM), vmem, vmem],
        out_specs=vmem,
        compiler_params=pltpu.CompilerParams(vmem_limit_bytes=32 * 2**20),
        name="shard_starts",
    )(row, totals, maps)


def gated_kernel(core_side, core_ref, reach_ref, start_ref, gate_ref, gain_ref, own_ref, other_ref):
    tokens = core_ref.shape[0]
    share = tokens // LOCAL
    side = core_side[0]
    for chip in range(LOCAL // 2):
        for ref, parity in ((own_ref, side), (other_ref, 1 - side)):
            rows = pl.ds((2 * chip + parity) * share, share)
            for h in range(HEADS):
                lanes = slice(h * DV, (h + 1) * DV)
                core = core_ref[rows, lanes] + mm_t(reach_ref[rows, lanes], start_ref[lanes, :])
                core = core * lax.rsqrt(jnp.mean(core * core, axis=-1, keepdims=True) + 1e-06)
                gate = gate_ref[rows, lanes].astype(f32)
                ref[chip * share : (chip + 1) * share, lanes] = (
                    core * gain_ref[...] * (gate / (1.0 + jnp.exp(-gate)))
                ).astype(bf16)


def gated_halves(side, core, reach, starts, gate, gain):
    tokens = core.shape[0]
    vmem = pl.BlockSpec(memory_space=pltpu.VMEM)
    half = jax.ShapeDtypeStruct((tokens // 2, HEADS * DV), bf16)
    return pl.pallas_call(
        gated_kernel,
        out_shape=(half, half),
        in_specs=[pl.BlockSpec(memory_space=pltpu.SMEM)] + [vmem] * 5,
        out_specs=(vmem, vmem),
        compiler_params=pltpu.CompilerParams(vmem_limit_bytes=32 * 2**20),
        name="gated_halves",
    )(side, core, reach, starts, gate, gain)


def project_kernel(own_ref, other_ref, own_weight, other_weight, out_ref):
    out_ref[...] = (mm(own_ref[...], own_weight[...]) + mm(other_ref[...], other_weight[...])).astype(bf16)


def project(own, other, own_weight, other_weight):
    rows, depth = own.shape
    width = own_weight.shape[1]
    tile = 512
    rows_spec = pl.BlockSpec((rows, depth), lambda i: (0, 0))
    weight_spec = pl.BlockSpec((depth, tile), lambda i: (0, i))
    return pl.pallas_call(
        project_kernel,
        out_shape=jax.ShapeDtypeStruct((rows, width), bf16),
        grid=(width // tile,),
        in_specs=[rows_spec, rows_spec, weight_spec, weight_spec],
        out_specs=pl.BlockSpec((rows, tile), lambda i: (0, i)),
        compiler_params=pltpu.CompilerParams(vmem_limit_bytes=32 * 2**20),
        name="project",
    )(own, other, own_weight, other_weight)


def residual_kernel(parts_ref, hidden_ref, gain_ref, state_ref, normed_ref):
    state = hidden_ref[...].astype(f32)
    for part in range(parts_ref.shape[0]):
        state = state + parts_ref[part].astype(f32)
    state_ref[...] = state
    normed = state * lax.rsqrt(jnp.mean(state * state, axis=-1, keepdims=True) + 1e-06) * gain_ref[...]
    for copy in range(normed_ref.shape[0]):
        normed_ref[copy] = normed.astype(bf16)


def residual(parts, hidden, gain):
    return pl.pallas_call(
        residual_kernel,
        out_shape=(
            jax.ShapeDtypeStruct(hidden.shape, f32),
            jax.ShapeDtypeStruct(parts.shape, bf16),
        ),
        compiler_params=pltpu.CompilerParams(vmem_limit_bytes=32 * 2**20),
        name="residual",
    )(parts, hidden, gain)


def routing_kernel(capacity, place_ref, index_ref, weight_ref, pick_ref, merge_ref, slot_s, share_s, wide_s):
    top, tokens = index_ref.shape
    groups = slot_s.shape[0]
    ids = lax.broadcasted_iota(jnp.int32, (groups, 1), 0) * LOCAL + place_ref[0]
    member = jnp.zeros((groups, tokens), f32)
    share = jnp.zeros((groups, tokens), f32)
    for j in range(top):
        hit = index_ref[j : j + 1, :] == ids
        member = jnp.where(hit, 1.0, member)
        share = jnp.where(hit, weight_ref[j : j + 1, :], share)
    earlier = lax.broadcasted_iota(jnp.int32, (tokens, tokens), 0) < lax.broadcasted_iota(
        jnp.int32, (tokens, tokens), 1
    )
    rank = mm(member, jnp.where(earlier, 1.0, 0.0))
    slot_s[...] = jnp.where(member > 0.0, rank, -1.0)
    share_s[...] = share
    several = 4
    span = several * capacity
    for i in range(groups // several):
        slot = slot_s[i * several : (i + 1) * several, :]
        part = share_s[i * several : (i + 1) * several, :]
        place = lax.broadcasted_iota(jnp.int32, (several, capacity, tokens), 1).astype(f32)
        hit = slot[:, None, :] == place
        pick_ref[i * span : (i + 1) * span, :] = (
            jnp.where(hit, 1.0, 0.0).reshape(span, tokens).astype(bf16)
        )
        wide_s[i * span : (i + 1) * span, :] = jnp.where(hit, part[:, None, :], 0.0).reshape(
            span, tokens
        )
    for i in range(groups * capacity // 128):
        merge_ref[:, i * 128 : (i + 1) * 128] = wide_s[i * 128 : (i + 1) * 128, :].T.astype(bf16)


def routing(place, index, weight, groups, capacity):
    top, tokens = index.shape
    slots = groups * capacity
    vmem = pl.BlockSpec(memory_space=pltpu.VMEM)
    return pl.pallas_call(
        lambda *refs: routing_kernel(capacity, *refs),
        out_shape=(
            jax.ShapeDtypeStruct((slots, tokens), bf16),
            jax.ShapeDtypeStruct((tokens, slots), bf16),
        ),
        in_specs=[pl.BlockSpec(memory_space=pltpu.SMEM), vmem, vmem],
        out_specs=(vmem, vmem),
        scratch_shapes=[
            pltpu.VMEM((groups, tokens), f32),
            pltpu.VMEM((groups, tokens), f32),
            pltpu.VMEM((slots, tokens), f32),
        ],
        compiler_params=pltpu.CompilerParams(vmem_limit_bytes=32 * 2**20),
        cost_estimate=pl.CostEstimate(flops=3 * 10**9, bytes_accessed=6 * 10**6, transcendentals=0),
        name="routing",
    )(place, index, weight)


def pick_kernel(pick_ref, own_ref, other_ref, out_ref):
    half = own_ref.shape[0]
    out_ref[...] = (mm(pick_ref[:, :half], own_ref[...]) + mm(pick_ref[:, half:], other_ref[...])).astype(bf16)


def pick_rows(pick, own, other):
    slots, tokens = pick.shape
    half, width = own.shape
    tile = 512
    half_spec = pl.BlockSpec((half, tile), lambda i: (0, i))
    return pl.pallas_call(
        pick_kernel,
        out_shape=jax.ShapeDtypeStruct((slots, width), bf16),
        grid=(width // tile,),
        in_specs=[pl.BlockSpec((slots, tokens), lambda i: (0, 0)), half_spec, half_spec],
        out_specs=pl.BlockSpec((slots, tile), lambda i: (0, i)),
        compiler_params=pltpu.CompilerParams(vmem_limit_bytes=32 * 2**20),
        name="pick_rows",
    )(pick, own, other)


def merge_kernel(merge_ref, rows_ref, out_ref):
    out_ref[...] = mm(merge_ref[...], rows_ref[...]).astype(bf16)


def merge_add_kernel(merge_ref, rows_ref, add_ref, out_ref):
    out_ref[...] = (mm(merge_ref[...], rows_ref[...]) + add_ref[...].astype(f32)).astype(bf16)


def merge_rows(merge, half, rows, *add):
    tokens, slots = merge.shape
    width = rows.shape[1]
    tile = 512
    out_spec = pl.BlockSpec((tokens // 2, tile), lambda i: (0, i))
    return pl.pallas_call(
        merge_add_kernel if add else merge_kernel,
        out_shape=jax.ShapeDtypeStruct((tokens // 2, width), bf16),
        grid=(width // tile,),
        in_specs=[
            pl.BlockSpec((tokens // 2, slots), lambda i: (half, 0)),
            pl.BlockSpec((slots, tile), lambda i: (0, i)),
        ]
        + [out_spec] * len(add),
        out_specs=out_spec,
        compiler_params=pltpu.CompilerParams(vmem_limit_bytes=32 * 2**20),
        name="merge_rows",
    )(merge, rows, *add)


def swap_cores(array):
    return lax.ppermute(array, "local", [(i, i ^ 1) for i in range(LOCAL)])


def across_chips(array):
    groups = [[side + 2 * chip for chip in range(LOCAL // 2)] for side in range(2)]
    return lax.all_to_all(
        array, "local", split_axis=0, concat_axis=0, tiled=True, axis_index_groups=groups
    )


def along_row(array):
    nodes = lax.axis_size("node")
    groups = [[row + z for z in range(NODE_ROW)] for row in range(0, nodes, NODE_ROW)]
    return lax.all_to_all(
        array, "node", split_axis=0, concat_axis=0, tiled=True, axis_index_groups=groups
    )


def across_rows(array):
    nodes = lax.axis_size("node")
    groups = [[row + z for row in range(0, nodes, NODE_ROW)] for z in range(NODE_ROW)]
    return lax.all_to_all(
        array, "node", split_axis=0, concat_axis=0, tiled=True, axis_index_groups=groups
    )


def across_nodes(array):
    return lax.all_to_all(array, "node", split_axis=0, concat_axis=0, tiled=True)


def local(
    hidden_in, queries, key_vectors, values, out_gate, log_decay, write_rate, norm_gain,
    out_weight, post_gain, expert_index, route_weight, expert_gate_up, expert_down,
):
    node_count = lax.axis_size("node")
    local_index = lax.axis_index("local")
    side = local_index % 2
    tokens, top = expert_index.shape
    chips = LOCAL // 2
    share = tokens // LOCAL
    width = hidden_in.shape[1]
    capacity = 6 * tokens * top // (5 * node_count * LOCAL)
    side_array = side.astype(jnp.int32).reshape(1)

    other_weight = swap_cores(out_weight)

    def by_side(array):
        split = array.T.reshape(top, chips, 2, share)
        split = jnp.where(side == 0, split, split[:, :, ::-1])
        return split.transpose(0, 2, 1, 3).reshape(top, tokens)

    pick, merge = routing(
        local_index.astype(jnp.int32).reshape(1), by_side(expert_index), by_side(route_weight),
        node_count, capacity,
    )

    payload, cum, inner, value_rows, starts = shard_maps(key_vectors, values, log_decay.T, write_rate.T)
    maps = along_row(payload)
    core, reach = block_reads(queries, key_vectors, cum, inner, value_rows, starts)
    maps, core, reach, pick, merge = lax.optimization_barrier((maps, core, reach, pick, merge))
    totals = across_rows(row_total(maps, node_count // NODE_ROW))
    row = (lax.axis_index("node") // NODE_ROW).astype(jnp.int32).reshape(1)
    carried = along_row(shard_starts(row, totals, maps)).reshape(HEADS * DV, DK)
    own_half, other_half = gated_halves(
        side_array, core, reach, carried, out_gate, norm_gain.reshape(1, DV)
    )
    partial = project(own_half, swap_cores(other_half), out_weight, other_weight)
    parts = across_chips(partial.reshape(chips, share, width))
    hidden_state, normed = residual(parts, hidden_in, post_gain.reshape(1, width))
    own_rows = across_chips(normed).reshape(chips * share, width)
    rows = pick_rows(pick, own_rows, swap_cores(own_rows)).reshape(node_count, capacity, width)
    rows = across_nodes(rows).reshape(node_count * capacity, width)
    gate_up = jnp.dot(rows, expert_gate_up[0], preferred_element_type=f32)
    half_width = gate_up.shape[1] // 2
    hidden_rows = (jax.nn.silu(gate_up[:, :half_width]) * gate_up[:, half_width:]).astype(bf16)
    results = jnp.dot(hidden_rows, expert_down[0], preferred_element_type=f32).astype(bf16)
    returned = across_nodes(results.reshape(node_count, capacity, width)).reshape(
        node_count * capacity, width
    )
    given = swap_cores(merge_rows(merge, 1, returned))
    summed = merge_rows(merge, 0, returned, given)
    arrived = across_chips(summed.reshape(chips, share, width))
    return (hidden_state + jnp.sum(arrived.astype(f32), axis=0)).astype(bf16)


def solution(mesh):
    return jax.shard_map(
        local,
        mesh=mesh,
        in_specs=(
            P(("node", "local"), None),
            P("node", "local"),
            P("node", "local"),
            P("node", "local"),
            P("node", "local"),
            P("node", "local"),
            P("node", "local"),
            P(),
            P("local", None),
            P(),
            P("node", None),
            P("node", None),
            P(("node", "local"), None, None),
            P(("node", "local"), None, None),
        ),
        out_specs=P(("node", "local"), None),
        check_vma=False,
    )
```

```python
import jax
import jax.numpy as jnp
from jax import lax
from jax.experimental import pallas as pl
from jax.experimental.pallas import tpu as pltpu
from jax.sharding import PartitionSpec as P

DK = 128
DV = 128
HEADS = 4
BLOCK = 64
STACK = HEADS * BLOCK
SPLIT = 2
NODE_ROW = 8
LOCAL = 8

f32 = jnp.float32
bf16 = jnp.bfloat16


def mm(a, b):
    return jnp.dot(a.astype(bf16), b.astype(bf16), preferred_element_type=f32)


def mm_t(a, b):
    return lax.dot_general(
        a.astype(bf16), b.astype(bf16), (((1,), (1,)), ((), ())), preferred_element_type=f32
    )


def t_mm(a, b):
    return lax.dot_general(
        a.astype(bf16), b.astype(bf16), (((0,), (0,)), ((), ())), preferred_element_type=f32
    )


def stack_rows(pieces):
    return jnp.concatenate(pieces, axis=0)


def head_column(columns):
    return stack_rows([columns[:, h : h + 1] for h in range(HEADS)])


def unit_scale(rows):
    wide = rows.astype(f32)
    return lax.rsqrt(jnp.sum(wide * wide, axis=-1, keepdims=True) + 1e-06)


def stacked_keys(key_ref, rows):
    keys = key_ref[rows, :]
    pair = [keys[:, :DK], keys[:, DK:]]
    scales = [unit_scale(p) for p in pair]
    return (
        stack_rows([pair[0], pair[0], pair[1], pair[1]]),
        stack_rows([scales[0], scales[0], scales[1], scales[1]]),
    )


def grid_places():
    row = lax.broadcasted_iota(jnp.int32, (STACK, STACK), 0)
    col = lax.broadcasted_iota(jnp.int32, (STACK, STACK), 1)
    return row, col, (row // BLOCK) == (col // BLOCK)


def as_row(column, row, col):
    return jnp.sum(jnp.where(row == col, column, 0.0), axis=0, keepdims=True)


def maps_kernel(
    key_ref, value_ref, decay_ref, rate_ref,
    payload_ref, cum_ref, inner_ref, values_ref, starts_ref,
    rate_s, tail_s, state_s, values_s,
):
    tokens = key_ref.shape[0]
    blocks = tokens // BLOCK
    lane = lax.broadcasted_iota(jnp.int32, (HEADS, tokens), 1) % BLOCK
    total = decay_ref[...]
    step = 1
    while step < BLOCK:
        total = total + jnp.where(lane >= step, pltpu.roll(total, step, 1), 0.0)
        step *= 2
    cum_ref[...] = total.T
    rate_s[...] = rate_ref[...].T

    def one_block(b):
        rows = pl.ds(b * BLOCK, BLOCK)
        row, col, same = grid_places()
        keys, scale = stacked_keys(key_ref, rows)
        cum = cum_ref[rows, :]
        cum_col = head_column(cum)
        rate_col = head_column(rate_s[rows, :])
        last_col = stack_rows(
            [jnp.broadcast_to(cum[BLOCK - 1 : BLOCK, h : h + 1], (BLOCK, 1)) for h in range(HEADS)]
        )
        strict = jnp.logical_and(same, row > col)
        past = jnp.exp(cum_col) * scale
        onward = as_row(jnp.exp(-cum_col) * scale, row, col)
        power = jnp.where(strict, mm_t(keys, keys) * ((-rate_col * past) * onward), 0.0)
        raw = value_ref[rows, :]
        wide = keys.astype(f32)
        answer = jnp.concatenate(
            [
                rate_col * stack_rows([raw[:, h * DV : (h + 1) * DV] for h in range(HEADS)]).astype(f32),
                (rate_col * past) * wide,
            ],
            axis=1,
        )
        return rows, power, answer, (jnp.exp(last_col - cum_col) * scale) * wide

    def finish(b, answer, tail):
        values_s[b] = answer[:, :DV]
        values_ref[b] = answer[:, :DV].astype(bf16)
        inner_ref[b] = answer[:, DV:].astype(bf16)
        tail_s[b] = tail.astype(bf16)

    for first in range(0, blocks, 4):
        group = range(first, first + 4)
        made = [one_block(b) for b in group]
        powers = [m[1] for m in made]
        answers = [m[2] for m in made]
        reach = 1
        while reach < BLOCK:
            answers = [a + mm(p, a) for p, a in zip(powers, answers)]
            reach *= 2
            if reach < BLOCK:
                powers = [mm(p, p) for p in powers]
        for b, a, m in zip(group, answers, made):
            finish(b, a, m[3])

    place = lax.broadcasted_iota(jnp.int32, (DK, DV + DK), 0)
    lane_place = lax.broadcasted_iota(jnp.int32, (DK, DV + DK), 1)
    for h in range(HEADS):
        state_s[h] = jnp.where(lane_place == place + DV, 1.0, 0.0)

    def advance(b, carry):
        last = cum_ref[pl.ds(b * BLOCK + BLOCK - 1, 1), :]
        parts = [slice(h * BLOCK, (h + 1) * BLOCK) for h in range(HEADS)]
        states = [state_s[h] for h in range(HEADS)]
        rounded = [state.astype(bf16) for state in states]
        changes = [mm(inner_ref[b, part, :], now) for part, now in zip(parts, rounded)]
        given = [
            jnp.concatenate([values_s[b, part, :] - change[:, :DV], -change[:, DV:]], axis=1)
            for part, change in zip(parts, changes)
        ]
        added = [t_mm(tail_s[b, part, :], rows) for part, rows in zip(parts, given)]
        for h in range(HEADS):
            starts_ref[b, h] = rounded[h]
            state_s[h] = jnp.exp(last[:, h : h + 1]) * states[h] + added[h]
        return carry

    lax.fori_loop(0, blocks, advance, 0, unroll=True)
    share = DV // SPLIT
    for h in range(HEADS):
        state = state_s[h]
        inject = state[:, :DV].T.astype(bf16)
        move = state[:, DV:].T.astype(bf16)
        for s in range(SPLIT):
            payload_ref[h * SPLIT + s, :DK, :] = move
            payload_ref[h * SPLIT + s, DK:, :] = inject[s * share : (s + 1) * share, :]


def shard_maps(keys, values, decay, rate):
    tokens = keys.shape[0]
    blocks = tokens // BLOCK
    return pl.pallas_call(
        maps_kernel,
        out_shape=(
            jax.ShapeDtypeStruct((HEADS * SPLIT, DK + DV // SPLIT, DK), bf16),
            jax.ShapeDtypeStruct((tokens, HEADS), f32),
            jax.ShapeDtypeStruct((blocks, STACK, DK), bf16),
            jax.ShapeDtypeStruct((blocks, STACK, DV), bf16),
            jax.ShapeDtypeStruct((blocks, HEADS, DK, DV + DK), bf16),
        ),
        scratch_shapes=[
            pltpu.VMEM((tokens, HEADS), f32),
            pltpu.VMEM((blocks, STACK, DK), bf16),
            pltpu.VMEM((HEADS, DK, DV + DK), f32),
            pltpu.VMEM((blocks, STACK, DV), f32),
        ],
        compiler_params=pltpu.CompilerParams(vmem_limit_bytes=60 * 2**20),
        name="shard_maps",
    )(keys, values, decay, rate)


def reads_kernel(query_ref, key_ref, cum_ref, inner_ref, values_ref, starts_ref, core_ref, reach_ref):
    blocks = query_ref.shape[0] // BLOCK

    def one_block(b):
        rows = pl.ds(b * BLOCK, BLOCK)
        row, col, same = grid_places()
        keys, scale = stacked_keys(key_ref, rows)
        queries, query_scale = stacked_keys(query_ref, rows)
        query_scale = query_scale * DK ** (-0.5)
        cum_col = head_column(cum_ref[rows, :])
        inclusive = jnp.logical_and(same, row >= col)
        past = jnp.exp(cum_col) * query_scale
        onward = as_row(jnp.exp(-cum_col) * scale, row, col)
        attention = jnp.where(inclusive, mm_t(queries, keys) * (past * onward), 0.0)
        both = mm(attention, jnp.concatenate([values_ref[b], inner_ref[b]], axis=1))
        emitter = (past * queries.astype(f32) - both[:, DV:]).astype(bf16)
        for h in range(HEADS):
            part = slice(h * BLOCK, (h + 1) * BLOCK)
            read = mm(emitter[part, :], starts_ref[b, h])
            core_ref[rows, h * DV : (h + 1) * DV] = both[part, :DV] + read[:, :DV]
            reach_ref[rows, h * DK : (h + 1) * DK] = read[:, DV:].astype(bf16)

    for b in range(blocks):
        one_block(b)


def block_reads(queries, keys, cum, inner, values, starts):
    tokens = keys.shape[0]
    return pl.pallas_call(
        reads_kernel,
        out_shape=(
            jax.ShapeDtypeStruct((tokens, HEADS * DV), f32),
            jax.ShapeDtypeStruct((tokens, HEADS * DK), bf16),
        ),
        compiler_params=pltpu.CompilerParams(vmem_limit_bytes=60 * 2**20),
        cost_estimate=pl.CostEstimate(flops=2 * 10**9, bytes_accessed=8 * 10**6, transcendentals=10**6),
        name="block_reads",
    )(queries, keys, cum, inner, values, starts)


def step(state, move):
    rows = state.shape[0]
    high = state.astype(bf16)
    low = (state - high.astype(f32)).astype(bf16)
    moved = jnp.dot(jnp.concatenate([high, low], axis=0), move, preferred_element_type=f32)
    return moved[:rows] + moved[rows:]


def row_total_kernel(maps_ref, total_ref):
    total = maps_ref[0].astype(f32)
    for k in range(1, maps_ref.shape[0]):
        moved = step(total, maps_ref[k, :DK, :])
        total = jnp.concatenate([moved[:DK], moved[DK:] + maps_ref[k, DK:, :].astype(f32)], axis=0)
    for copy in range(total_ref.shape[0]):
        total_ref[copy] = total.astype(bf16)


def row_total(maps, rows):
    return pl.pallas_call(
        row_total_kernel,
        out_shape=jax.ShapeDtypeStruct((rows,) + maps.shape[1:], bf16),
        compiler_params=pltpu.CompilerParams(vmem_limit_bytes=32 * 2**20),
        name="row_total",
    )(maps)


def starts_kernel(row_ref, totals_ref, maps_ref, start_ref):
    def apply(state, ref, k):
        return step(state, ref[k, :DK, :]) + ref[k, DK:, :].astype(f32)

    state = jnp.zeros(start_ref.shape[1:], f32)
    for k in range(totals_ref.shape[0] - 1):
        state = jnp.where(k < row_ref[0], apply(state, totals_ref, k), state)
    for k in range(maps_ref.shape[0]):
        start_ref[k] = state.astype(bf16)
        if k + 1 < maps_ref.shape[0]:
            state = apply(state, maps_ref, k)


def shard_starts(row, totals, maps):
    vmem = pl.BlockSpec(memory_space=pltpu.VMEM)
    return pl.pallas_call(
        starts_kernel,
        out_shape=jax.ShapeDtypeStruct((maps.shape[0], maps.shape[1] - DK, DK), bf16),
        in_specs=[pl.BlockSpec(memory_space=pltpu.SMEM), vmem, vmem],
        out_specs=vmem,
        compiler_params=pltpu.CompilerParams(vmem_limit_bytes=32 * 2**20),
        name="shard_starts",
    )(row, totals, maps)


def gated_kernel(
    core_side, core_ref, reach_ref, start_ref, gate_ref, gain_ref, own_ref, other_ref, gated_s
):
    share = core_ref.shape[0] // LOCAL
    lanes = [slice(h * DV, (h + 1) * DV) for h in range(HEADS)]
    reads = [mm_t(reach_ref[:, lane], start_ref[lane, :]) for lane in lanes]
    for lane, read in zip(lanes, reads):
        core = core_ref[:, lane] + read
        core = core * lax.rsqrt(jnp.mean(core * core, axis=-1, keepdims=True) + 1e-06)
        gate = gate_ref[:, lane].astype(f32)
        gated_s[:, lane] = (core * gain_ref[...] * (gate / (1.0 + jnp.exp(-gate)))).astype(bf16)
    side = core_side[0]
    for chip in range(LOCAL // 2):
        for ref, parity in ((own_ref, side), (other_ref, 1 - side)):
            first = pl.multiple_of((2 * chip + parity) * share, share)
            ref[chip * share : (chip + 1) * share, :] = gated_s[pl.ds(first, share), :]


def gated_halves(side, core, reach, starts, gate, gain):
    tokens = core.shape[0]
    vmem = pl.BlockSpec(memory_space=pltpu.VMEM)
    half = jax.ShapeDtypeStruct((tokens // 2, HEADS * DV), bf16)
    return pl.pallas_call(
        gated_kernel,
        out_shape=(half, half),
        in_specs=[pl.BlockSpec(memory_space=pltpu.SMEM)] + [vmem] * 5,
        out_specs=(vmem, vmem),
        scratch_shapes=[pltpu.VMEM((tokens, HEADS * DV), bf16)],
        compiler_params=pltpu.CompilerParams(vmem_limit_bytes=60 * 2**20),
        name="gated_halves",
    )(side, core, reach, starts, gate, gain)


def project_kernel(own_ref, other_ref, own_weight, other_weight, out_ref):
    out_ref[...] = (mm(own_ref[...], own_weight[...]) + mm(other_ref[...], other_weight[...])).astype(bf16)


def project(own, other, own_weight, other_weight):
    rows, depth = own.shape
    width = own_weight.shape[1]
    tile = width // 2
    rows_spec = pl.BlockSpec((rows, depth), lambda i: (0, 0))
    weight_spec = pl.BlockSpec((depth, tile), lambda i: (0, i))
    return pl.pallas_call(
        project_kernel,
        out_shape=jax.ShapeDtypeStruct((rows, width), bf16),
        grid=(width // tile,),
        in_specs=[rows_spec, rows_spec, weight_spec, weight_spec],
        out_specs=pl.BlockSpec((rows, tile), lambda i: (0, i)),
        compiler_params=pltpu.CompilerParams(vmem_limit_bytes=60 * 2**20),
        name="project",
    )(own, other, own_weight, other_weight)


def residual_kernel(parts_ref, hidden_ref, gain_ref, state_ref, normed_ref):
    state = hidden_ref[...].astype(f32)
    for part in range(parts_ref.shape[0]):
        state = state + parts_ref[part].astype(f32)
    state_ref[...] = state
    normed = state * lax.rsqrt(jnp.mean(state * state, axis=-1, keepdims=True) + 1e-06) * gain_ref[...]
    for copy in range(normed_ref.shape[0]):
        normed_ref[copy] = normed.astype(bf16)


def residual(parts, hidden, gain):
    return pl.pallas_call(
        residual_kernel,
        out_shape=(
            jax.ShapeDtypeStruct(hidden.shape, f32),
            jax.ShapeDtypeStruct(parts.shape, bf16),
        ),
        compiler_params=pltpu.CompilerParams(vmem_limit_bytes=32 * 2**20),
        name="residual",
    )(parts, hidden, gain)


def routing_kernel(capacity, place_ref, index_ref, weight_ref, pick_ref, merge_ref, slot_s, share_s, wide_s):
    top, tokens = index_ref.shape
    groups = slot_s.shape[0]
    ids = lax.broadcasted_iota(jnp.int32, (groups, 1), 0) * LOCAL + place_ref[0]
    member = jnp.zeros((groups, tokens), f32)
    share = jnp.zeros((groups, tokens), f32)
    for j in range(top):
        hit = index_ref[j : j + 1, :] == ids
        member = jnp.where(hit, 1.0, member)
        share = jnp.where(hit, weight_ref[j : j + 1, :], share)
    earlier = lax.broadcasted_iota(jnp.int32, (tokens, tokens), 0) < lax.broadcasted_iota(
        jnp.int32, (tokens, tokens), 1
    )
    rank = mm(member, jnp.where(earlier, 1.0, 0.0))
    slot_s[...] = jnp.where(member > 0.0, rank, -1.0)
    share_s[...] = share
    several = 4
    span = several * capacity
    for i in range(groups // several):
        slot = slot_s[i * several : (i + 1) * several, :]
        part = share_s[i * several : (i + 1) * several, :]
        place = lax.broadcasted_iota(jnp.int32, (several, capacity, tokens), 1).astype(f32)
        hit = slot[:, None, :] == place
        pick_ref[i * span : (i + 1) * span, :] = (
            jnp.where(hit, 1.0, 0.0).reshape(span, tokens).astype(bf16)
        )
        wide_s[i * span : (i + 1) * span, :] = jnp.where(hit, part[:, None, :], 0.0).reshape(
            span, tokens
        )
    for i in range(groups * capacity // 128):
        merge_ref[:, i * 128 : (i + 1) * 128] = wide_s[i * 128 : (i + 1) * 128, :].T.astype(bf16)


def routing(place, index, weight, groups, capacity):
    top, tokens = index.shape
    slots = groups * capacity
    vmem = pl.BlockSpec(memory_space=pltpu.VMEM)
    return pl.pallas_call(
        lambda *refs: routing_kernel(capacity, *refs),
        out_shape=(
            jax.ShapeDtypeStruct((slots, tokens), bf16),
            jax.ShapeDtypeStruct((tokens, slots), bf16),
        ),
        in_specs=[pl.BlockSpec(memory_space=pltpu.SMEM), vmem, vmem],
        out_specs=(vmem, vmem),
        scratch_shapes=[
            pltpu.VMEM((groups, tokens), f32),
            pltpu.VMEM((groups, tokens), f32),
            pltpu.VMEM((slots, tokens), f32),
        ],
        compiler_params=pltpu.CompilerParams(vmem_limit_bytes=32 * 2**20),
        cost_estimate=pl.CostEstimate(flops=3 * 10**9, bytes_accessed=6 * 10**6, transcendentals=0),
        name="routing",
    )(place, index, weight)


def pick_kernel(pick_ref, own_ref, other_ref, out_ref):
    half = own_ref.shape[0]
    out_ref[...] = (mm(pick_ref[:, :half], own_ref[...]) + mm(pick_ref[:, half:], other_ref[...])).astype(bf16)


def pick_rows(pick, own, other):
    slots, tokens = pick.shape
    half, width = own.shape
    tile = 1024
    half_spec = pl.BlockSpec((half, tile), lambda i: (0, i))
    return pl.pallas_call(
        pick_kernel,
        out_shape=jax.ShapeDtypeStruct((slots, width), bf16),
        grid=(width // tile,),
        in_specs=[pl.BlockSpec((slots, tokens), lambda i: (0, 0)), half_spec, half_spec],
        out_specs=pl.BlockSpec((slots, tile), lambda i: (0, i)),
        compiler_params=pltpu.CompilerParams(vmem_limit_bytes=32 * 2**20),
        name="pick_rows",
    )(pick, own, other)


def merge_kernel(merge_ref, rows_ref, out_ref):
    out_ref[...] = mm(merge_ref[...], rows_ref[...]).astype(bf16)


def merge_rows(merge, half, rows):
    tokens, slots = merge.shape
    width = rows.shape[1]
    return pl.pallas_call(
        merge_kernel,
        out_shape=jax.ShapeDtypeStruct((tokens // 2, width), bf16),
        grid=(1,),
        in_specs=[
            pl.BlockSpec((tokens // 2, slots), lambda i: (half, 0)),
            pl.BlockSpec((slots, width), lambda i: (0, 0)),
        ],
        out_specs=pl.BlockSpec((tokens // 2, width), lambda i: (0, 0)),
        compiler_params=pltpu.CompilerParams(vmem_limit_bytes=32 * 2**20),
        cost_estimate=pl.CostEstimate(
            flops=tokens * slots * width, bytes_accessed=5 * 10**6, transcendentals=0
        ),
        name="merge_rows",
    )(merge, rows)


def swap_cores(array):
    return lax.ppermute(array, "local", [(i, i ^ 1) for i in range(LOCAL)])


def across_chips(array):
    groups = [[side + 2 * chip for chip in range(LOCAL // 2)] for side in range(2)]
    return lax.all_to_all(
        array, "local", split_axis=0, concat_axis=0, tiled=True, axis_index_groups=groups
    )


def along_row(array):
    nodes = lax.axis_size("node")
    groups = [[row + z for z in range(NODE_ROW)] for row in range(0, nodes, NODE_ROW)]
    return lax.all_to_all(
        array, "node", split_axis=0, concat_axis=0, tiled=True, axis_index_groups=groups
    )


def across_rows(array):
    nodes = lax.axis_size("node")
    groups = [[row + z for row in range(0, nodes, NODE_ROW)] for z in range(NODE_ROW)]
    return lax.all_to_all(
        array, "node", split_axis=0, concat_axis=0, tiled=True, axis_index_groups=groups
    )


def across_nodes(array):
    return lax.all_to_all(array, "node", split_axis=0, concat_axis=0, tiled=True)


def local(
    hidden_in, queries, key_vectors, values, out_gate, log_decay, write_rate, norm_gain,
    out_weight, post_gain, expert_index, route_weight, expert_gate_up, expert_down,
):
    node_count = lax.axis_size("node")
    local_index = lax.axis_index("local")
    side = local_index % 2
    tokens, top = expert_index.shape
    chips = LOCAL // 2
    share = tokens // LOCAL
    width = hidden_in.shape[1]
    capacity = 6 * tokens * top // (5 * node_count * LOCAL)
    side_array = side.astype(jnp.int32).reshape(1)

    other_weight = swap_cores(out_weight)

    def by_side(array):
        split = array.T.reshape(top, chips, 2, share)
        split = jnp.where(side == 0, split, split[:, :, ::-1])
        return split.transpose(0, 2, 1, 3).reshape(top, tokens)

    pick, merge = routing(
        local_index.astype(jnp.int32).reshape(1), by_side(expert_index), by_side(route_weight),
        node_count, capacity,
    )

    payload, cum, inner, value_rows, starts = shard_maps(key_vectors, values, log_decay.T, write_rate.T)
    maps = along_row(payload)
    core, reach = block_reads(queries, key_vectors, cum, inner, value_rows, starts)
    maps, core, reach, pick, merge = lax.optimization_barrier((maps, core, reach, pick, merge))
    totals = across_rows(row_total(maps, node_count // NODE_ROW))
    row = (lax.axis_index("node") // NODE_ROW).astype(jnp.int32).reshape(1)
    carried = along_row(shard_starts(row, totals, maps)).reshape(HEADS * DV, DK)
    own_half, other_half = gated_halves(
        side_array, core, reach, carried, out_gate, norm_gain.reshape(1, DV)
    )
    partial = project(own_half, swap_cores(other_half), out_weight, other_weight)
    parts = across_chips(partial.reshape(chips, share, width))
    hidden_state, normed = residual(parts, hidden_in, post_gain.reshape(1, width))
    own_rows = across_chips(normed).reshape(chips * share, width)
    rows = pick_rows(pick, own_rows, swap_cores(own_rows)).reshape(node_count, capacity, width)
    rows = across_nodes(rows).reshape(node_count * capacity, width)
    gate_up = jnp.dot(rows, expert_gate_up[0], preferred_element_type=f32)
    half_width = gate_up.shape[1] // 2
    hidden_rows = (jax.nn.silu(gate_up[:, :half_width]) * gate_up[:, half_width:]).astype(bf16)
    results = jnp.dot(hidden_rows, expert_down[0], preferred_element_type=f32).astype(bf16)
    returned = across_nodes(results.reshape(node_count, capacity, width)).reshape(
        node_count * capacity, width
    )
    given = swap_cores(merge_rows(merge, 1, returned))
    kept = merge_rows(merge, 0, returned)
    summed = (kept.astype(f32) + given.astype(f32)).astype(bf16)
    arrived = across_chips(summed.reshape(chips, share, width))
    return (hidden_state + jnp.sum(arrived.astype(f32), axis=0)).astype(bf16)


def solution(mesh):
    return jax.shard_map(
        local,
        mesh=mesh,
        in_specs=(
            P(("node", "local"), None),
            P("node", "local"),
            P("node", "local"),
            P("node", "local"),
            P("node", "local"),
            P("node", "local"),
            P("node", "local"),
            P(),
            P("local", None),
            P(),
            P("node", None),
            P("node", None),
            P(("node", "local"), None, None),
            P(("node", "local"), None, None),
        ),
        out_specs=P(("node", "local"), None),
        check_vma=False,
    )
```

```python
import jax
import jax.numpy as jnp
from jax import lax
from jax.experimental import pallas as pl
from jax.experimental.pallas import tpu as pltpu
from jax.sharding import PartitionSpec as P

DK = 128
DV = 128
HEADS = 4
BLOCK = 64
STACK = HEADS * BLOCK
SPLIT = 2
NODE_ROW = 8
LOCAL = 8

f32 = jnp.float32
bf16 = jnp.bfloat16


def mm(a, b):
    return jnp.dot(a.astype(bf16), b.astype(bf16), preferred_element_type=f32)


def mm_t(a, b):
    return lax.dot_general(
        a.astype(bf16), b.astype(bf16), (((1,), (1,)), ((), ())), preferred_element_type=f32
    )


def t_mm(a, b):
    return lax.dot_general(
        a.astype(bf16), b.astype(bf16), (((0,), (0,)), ((), ())), preferred_element_type=f32
    )


def stack_rows(pieces):
    return jnp.concatenate(pieces, axis=0)


def head_column(columns):
    return stack_rows([columns[:, h : h + 1] for h in range(HEADS)])


def unit_scale(rows):
    wide = rows.astype(f32)
    return lax.rsqrt(jnp.sum(wide * wide, axis=-1, keepdims=True) + 1e-06)


def stacked_keys(key_ref, rows):
    keys = key_ref[rows, :]
    pair = [keys[:, :DK], keys[:, DK:]]
    scales = [unit_scale(p) for p in pair]
    return (
        stack_rows([pair[0], pair[0], pair[1], pair[1]]),
        stack_rows([scales[0], scales[0], scales[1], scales[1]]),
    )


def grid_places():
    row = lax.broadcasted_iota(jnp.int32, (STACK, STACK), 0)
    col = lax.broadcasted_iota(jnp.int32, (STACK, STACK), 1)
    return row, col, (row // BLOCK) == (col // BLOCK)


def as_row(column, row, col):
    return jnp.sum(jnp.where(row == col, column, 0.0), axis=0, keepdims=True)


def maps_kernel(
    key_ref, value_ref, decay_ref, rate_ref,
    payload_ref, cum_ref, inner_ref, values_ref, starts_ref,
    rate_s, tail_s, state_s, values_s,
):
    tokens = key_ref.shape[0]
    blocks = tokens // BLOCK
    lane = lax.broadcasted_iota(jnp.int32, (HEADS, tokens), 1) % BLOCK
    total = decay_ref[...]
    step = 1
    while step < BLOCK:
        total = total + jnp.where(lane >= step, pltpu.roll(total, step, 1), 0.0)
        step *= 2
    cum_ref[...] = total.T
    rate_s[...] = rate_ref[...].T

    def one_block(b):
        rows = pl.ds(b * BLOCK, BLOCK)
        row, col, same = grid_places()
        keys, scale = stacked_keys(key_ref, rows)
        cum = cum_ref[rows, :]
        cum_col = head_column(cum)
        rate_col = head_column(rate_s[rows, :])
        last_col = stack_rows(
            [jnp.broadcast_to(cum[BLOCK - 1 : BLOCK, h : h + 1], (BLOCK, 1)) for h in range(HEADS)]
        )
        strict = jnp.logical_and(same, row > col)
        past = jnp.exp(cum_col) * scale
        onward = as_row(jnp.exp(-cum_col) * scale, row, col)
        power = jnp.where(strict, mm_t(keys, keys) * ((-rate_col * past) * onward), 0.0)
        raw = value_ref[rows, :]
        wide = keys.astype(f32)
        answer = jnp.concatenate(
            [
                rate_col * stack_rows([raw[:, h * DV : (h + 1) * DV] for h in range(HEADS)]).astype(f32),
                (rate_col * past) * wide,
            ],
            axis=1,
        )
        return rows, power, answer, (jnp.exp(last_col - cum_col) * scale) * wide

    def finish(b, answer, tail):
        values_s[b] = answer[:, :DV]
        values_ref[b] = answer[:, :DV].astype(bf16)
        inner_ref[b] = answer[:, DV:].astype(bf16)
        tail_s[b] = tail.astype(bf16)

    for first in range(0, blocks, 4):
        group = range(first, first + 4)
        made = [one_block(b) for b in group]
        powers = [m[1] for m in made]
        answers = [m[2] for m in made]
        reach = 1
        while reach < BLOCK:
            answers = [a + mm(p, a) for p, a in zip(powers, answers)]
            reach *= 2
            if reach < BLOCK:
                powers = [mm(p, p) for p in powers]
        for b, a, m in zip(group, answers, made):
            finish(b, a, m[3])

    place = lax.broadcasted_iota(jnp.int32, (DK, DV + DK), 0)
    lane_place = lax.broadcasted_iota(jnp.int32, (DK, DV + DK), 1)
    for h in range(HEADS):
        state_s[h] = jnp.where(lane_place == place + DV, 1.0, 0.0)

    def advance(b, carry):
        last = cum_ref[pl.ds(b * BLOCK + BLOCK - 1, 1), :]
        parts = [slice(h * BLOCK, (h + 1) * BLOCK) for h in range(HEADS)]
        states = [state_s[h] for h in range(HEADS)]
        rounded = [state.astype(bf16) for state in states]
        changes = [mm(inner_ref[b, part, :], now) for part, now in zip(parts, rounded)]
        given = [
            jnp.concatenate([values_s[b, part, :] - change[:, :DV], -change[:, DV:]], axis=1)
            for part, change in zip(parts, changes)
        ]
        added = [t_mm(tail_s[b, part, :], rows) for part, rows in zip(parts, given)]
        for h in range(HEADS):
            starts_ref[b, h] = rounded[h]
            state_s[h] = jnp.exp(last[:, h : h + 1]) * states[h] + added[h]
        return carry

    lax.fori_loop(0, blocks, advance, 0, unroll=True)
    share = DV // SPLIT
    for h in range(HEADS):
        state = state_s[h]
        inject = state[:, :DV].T.astype(bf16)
        move = state[:, DV:].T.astype(bf16)
        for s in range(SPLIT):
            payload_ref[h * SPLIT + s, :DK, :] = move
            payload_ref[h * SPLIT + s, DK:, :] = inject[s * share : (s + 1) * share, :]


def shard_maps(keys, values, decay, rate):
    tokens = keys.shape[0]
    blocks = tokens // BLOCK
    return pl.pallas_call(
        maps_kernel,
        out_shape=(
            jax.ShapeDtypeStruct((HEADS * SPLIT, DK + DV // SPLIT, DK), bf16),
            jax.ShapeDtypeStruct((tokens, HEADS), f32),
            jax.ShapeDtypeStruct((blocks, STACK, DK), bf16),
            jax.ShapeDtypeStruct((blocks, STACK, DV), bf16),
            jax.ShapeDtypeStruct((blocks, HEADS, DK, DV + DK), bf16),
        ),
        scratch_shapes=[
            pltpu.VMEM((tokens, HEADS), f32),
            pltpu.VMEM((blocks, STACK, DK), bf16),
            pltpu.VMEM((HEADS, DK, DV + DK), f32),
            pltpu.VMEM((blocks, STACK, DV), f32),
        ],
        compiler_params=pltpu.CompilerParams(vmem_limit_bytes=60 * 2**20),
        name="shard_maps",
    )(keys, values, decay, rate)


def reads_kernel(query_ref, key_ref, cum_ref, inner_ref, values_ref, starts_ref, core_ref, reach_ref):
    blocks = query_ref.shape[0] // BLOCK

    def one_block(b):
        rows = pl.ds(b * BLOCK, BLOCK)
        row, col, same = grid_places()
        keys, scale = stacked_keys(key_ref, rows)
        queries, query_scale = stacked_keys(query_ref, rows)
        query_scale = query_scale * DK ** (-0.5)
        cum_col = head_column(cum_ref[rows, :])
        inclusive = jnp.logical_and(same, row >= col)
        past = jnp.exp(cum_col) * query_scale
        onward = as_row(jnp.exp(-cum_col) * scale, row, col)
        attention = jnp.where(inclusive, mm_t(queries, keys) * (past * onward), 0.0)
        both = mm(attention, jnp.concatenate([values_ref[b], inner_ref[b]], axis=1))
        emitter = (past * queries.astype(f32) - both[:, DV:]).astype(bf16)
        for h in range(HEADS):
            part = slice(h * BLOCK, (h + 1) * BLOCK)
            read = mm(emitter[part, :], starts_ref[b, h])
            core_ref[rows, h * DV : (h + 1) * DV] = both[part, :DV] + read[:, :DV]
            reach_ref[rows, h * DK : (h + 1) * DK] = read[:, DV:].astype(bf16)

    for b in range(blocks):
        one_block(b)


def block_reads(queries, keys, cum, inner, values, starts):
    tokens = keys.shape[0]
    return pl.pallas_call(
        reads_kernel,
        out_shape=(
            jax.ShapeDtypeStruct((tokens, HEADS * DV), f32),
            jax.ShapeDtypeStruct((tokens, HEADS * DK), bf16),
        ),
        compiler_params=pltpu.CompilerParams(vmem_limit_bytes=60 * 2**20),
        cost_estimate=pl.CostEstimate(flops=2 * 10**9, bytes_accessed=8 * 10**6, transcendentals=10**6),
        name="block_reads",
    )(queries, keys, cum, inner, values, starts)


def step(state, move):
    rows = state.shape[0]
    high = state.astype(bf16)
    low = (state - high.astype(f32)).astype(bf16)
    moved = jnp.dot(jnp.concatenate([high, low], axis=0), move, preferred_element_type=f32)
    return moved[:rows] + moved[rows:]


def row_total_kernel(maps_ref, total_ref):
    total = maps_ref[0].astype(f32)
    for k in range(1, maps_ref.shape[0]):
        moved = step(total, maps_ref[k, :DK, :])
        total = jnp.concatenate([moved[:DK], moved[DK:] + maps_ref[k, DK:, :].astype(f32)], axis=0)
    for copy in range(total_ref.shape[0]):
        total_ref[copy] = total.astype(bf16)


def row_total(maps, rows):
    return pl.pallas_call(
        row_total_kernel,
        out_shape=jax.ShapeDtypeStruct((rows,) + maps.shape[1:], bf16),
        compiler_params=pltpu.CompilerParams(vmem_limit_bytes=32 * 2**20),
        name="row_total",
    )(maps)


def starts_kernel(row_ref, totals_ref, maps_ref, start_ref):
    def apply(state, ref, k):
        return step(state, ref[k, :DK, :]) + ref[k, DK:, :].astype(f32)

    state = jnp.zeros(start_ref.shape[1:], f32)
    for k in range(totals_ref.shape[0] - 1):
        state = jnp.where(k < row_ref[0], apply(state, totals_ref, k), state)
    for k in range(maps_ref.shape[0]):
        start_ref[k] = state.astype(bf16)
        if k + 1 < maps_ref.shape[0]:
            state = apply(state, maps_ref, k)


def shard_starts(row, totals, maps):
    vmem = pl.BlockSpec(memory_space=pltpu.VMEM)
    return pl.pallas_call(
        starts_kernel,
        out_shape=jax.ShapeDtypeStruct((maps.shape[0], maps.shape[1] - DK, DK), bf16),
        in_specs=[pl.BlockSpec(memory_space=pltpu.SMEM), vmem, vmem],
        out_specs=vmem,
        compiler_params=pltpu.CompilerParams(vmem_limit_bytes=32 * 2**20),
        name="shard_starts",
    )(row, totals, maps)


def gated_kernel(
    core_side, core_ref, reach_ref, start_ref, gate_ref, gain_ref, weight_hbm,
    own_ref, part_ref, gated_s, other_s, weight_s, arrival,
):
    fetch = pltpu.make_async_copy(weight_hbm, weight_s, arrival)
    fetch.start()
    share = core_ref.shape[0] // LOCAL
    lanes = [slice(h * DV, (h + 1) * DV) for h in range(HEADS)]
    reads = [mm_t(reach_ref[:, lane], start_ref[lane, :]) for lane in lanes]
    for lane, read in zip(lanes, reads):
        core = core_ref[:, lane] + read
        core = core * lax.rsqrt(jnp.mean(core * core, axis=-1, keepdims=True) + 1e-06)
        gate = gate_ref[:, lane].astype(f32)
        gated_s[:, lane] = (core * gain_ref[...] * (gate / (1.0 + jnp.exp(-gate)))).astype(bf16)
    side = core_side[0]
    for chip in range(LOCAL // 2):
        for ref, parity in ((own_ref, side), (other_s, 1 - side)):
            first = pl.multiple_of((2 * chip + parity) * share, share)
            ref[chip * share : (chip + 1) * share, :] = gated_s[pl.ds(first, share), :]
    fetch.wait()
    part_ref[...] = mm(other_s[...], weight_s[...]).astype(bf16)


def gated_part(side, core, reach, starts, gate, gain, weight):
    tokens, depth = core.shape
    half = tokens // 2
    vmem = pl.BlockSpec(memory_space=pltpu.VMEM)
    return pl.pallas_call(
        gated_kernel,
        out_shape=(
            jax.ShapeDtypeStruct((half, depth), bf16),
            jax.ShapeDtypeStruct((half, weight.shape[1]), bf16),
        ),
        in_specs=[pl.BlockSpec(memory_space=pltpu.SMEM)]
        + [vmem] * 5
        + [pl.BlockSpec(memory_space=pl.ANY)],
        out_specs=(vmem, vmem),
        scratch_shapes=[
            pltpu.VMEM((tokens, depth), bf16),
            pltpu.VMEM((half, depth), bf16),
            pltpu.VMEM(weight.shape, bf16),
            pltpu.SemaphoreType.DMA,
        ],
        compiler_params=pltpu.CompilerParams(vmem_limit_bytes=60 * 2**20),
        name="gated_part",
    )(side, core, reach, starts, gate, gain, weight)


def project_kernel(rows_ref, weight_ref, out_ref):
    out_ref[...] = mm(rows_ref[...], weight_ref[...]).astype(bf16)


def project(rows, weight):
    return pl.pallas_call(
        project_kernel,
        out_shape=jax.ShapeDtypeStruct((rows.shape[0], weight.shape[1]), bf16),
        compiler_params=pltpu.CompilerParams(vmem_limit_bytes=32 * 2**20),
        cost_estimate=pl.CostEstimate(
            flops=2 * rows.size * weight.shape[1], bytes_accessed=4 * 10**6, transcendentals=0
        ),
        name="project",
    )(rows, weight)


def residual_kernel(parts_ref, hidden_ref, gain_ref, state_ref, normed_ref):
    state = hidden_ref[...].astype(f32)
    for part in range(parts_ref.shape[0]):
        state = state + parts_ref[part].astype(f32)
    state_ref[...] = state
    normed = state * lax.rsqrt(jnp.mean(state * state, axis=-1, keepdims=True) + 1e-06) * gain_ref[...]
    for copy in range(normed_ref.shape[0]):
        normed_ref[copy] = normed.astype(bf16)


def residual(parts, hidden, gain):
    return pl.pallas_call(
        residual_kernel,
        out_shape=(
            jax.ShapeDtypeStruct(hidden.shape, f32),
            jax.ShapeDtypeStruct(parts.shape, bf16),
        ),
        compiler_params=pltpu.CompilerParams(vmem_limit_bytes=32 * 2**20),
        name="residual",
    )(parts, hidden, gain)


def routing_kernel(capacity, place_ref, index_ref, weight_ref, pick_ref, merge_ref, slot_s, share_s, wide_s):
    top, tokens = index_ref.shape
    groups = slot_s.shape[0]
    ids = lax.broadcasted_iota(jnp.int32, (groups, 1), 0) * LOCAL + place_ref[0]
    member = jnp.zeros((groups, tokens), f32)
    share = jnp.zeros((groups, tokens), f32)
    for j in range(top):
        hit = index_ref[j : j + 1, :] == ids
        member = jnp.where(hit, 1.0, member)
        share = jnp.where(hit, weight_ref[j : j + 1, :], share)
    earlier = lax.broadcasted_iota(jnp.int32, (tokens, tokens), 0) < lax.broadcasted_iota(
        jnp.int32, (tokens, tokens), 1
    )
    rank = mm(member, jnp.where(earlier, 1.0, 0.0))
    slot_s[...] = jnp.where(member > 0.0, rank, -1.0)
    share_s[...] = share
    several = 4
    span = several * capacity
    for i in range(groups // several):
        slot = slot_s[i * several : (i + 1) * several, :]
        part = share_s[i * several : (i + 1) * several, :]
        place = lax.broadcasted_iota(jnp.int32, (several, capacity, tokens), 1).astype(f32)
        hit = slot[:, None, :] == place
        pick_ref[i * span : (i + 1) * span, :] = (
            jnp.where(hit, 1.0, 0.0).reshape(span, tokens).astype(bf16)
        )
        wide_s[i * span : (i + 1) * span, :] = jnp.where(hit, part[:, None, :], 0.0).reshape(
            span, tokens
        )
    for i in range(groups * capacity // 128):
        merge_ref[:, i * 128 : (i + 1) * 128] = wide_s[i * 128 : (i + 1) * 128, :].T.astype(bf16)


def routing(place, index, weight, groups, capacity):
    top, tokens = index.shape
    slots = groups * capacity
    vmem = pl.BlockSpec(memory_space=pltpu.VMEM)
    return pl.pallas_call(
        lambda *refs: routing_kernel(capacity, *refs),
        out_shape=(
            jax.ShapeDtypeStruct((slots, tokens), bf16),
            jax.ShapeDtypeStruct((tokens, slots), bf16),
        ),
        in_specs=[pl.BlockSpec(memory_space=pltpu.SMEM), vmem, vmem],
        out_specs=(vmem, vmem),
        scratch_shapes=[
            pltpu.VMEM((groups, tokens), f32),
            pltpu.VMEM((groups, tokens), f32),
            pltpu.VMEM((slots, tokens), f32),
        ],
        compiler_params=pltpu.CompilerParams(vmem_limit_bytes=32 * 2**20),
        cost_estimate=pl.CostEstimate(flops=3 * 10**9, bytes_accessed=6 * 10**6, transcendentals=0),
        name="routing",
    )(place, index, weight)


def pick_kernel(pick_ref, own_ref, other_ref, out_ref):
    half = own_ref.shape[0]
    out_ref[...] = (mm(pick_ref[:, :half], own_ref[...]) + mm(pick_ref[:, half:], other_ref[...])).astype(bf16)


def pick_rows(pick, own, other):
    slots, tokens = pick.shape
    half, width = own.shape
    tile = 1024
    half_spec = pl.BlockSpec((half, tile), lambda i: (0, i))
    return pl.pallas_call(
        pick_kernel,
        out_shape=jax.ShapeDtypeStruct((slots, width), bf16),
        grid=(width // tile,),
        in_specs=[pl.BlockSpec((slots, tokens), lambda i: (0, 0)), half_spec, half_spec],
        out_specs=pl.BlockSpec((slots, tile), lambda i: (0, i)),
        compiler_params=pltpu.CompilerParams(vmem_limit_bytes=32 * 2**20),
        name="pick_rows",
    )(pick, own, other)


def merge_kernel(merge_ref, rows_ref, out_ref):
    out_ref[...] = mm(merge_ref[...], rows_ref[...]).astype(bf16)


def merge_rows(merge, half, rows):
    tokens, slots = merge.shape
    width = rows.shape[1]
    return pl.pallas_call(
        merge_kernel,
        out_shape=jax.ShapeDtypeStruct((tokens // 2, width), bf16),
        grid=(1,),
        in_specs=[
            pl.BlockSpec((tokens // 2, slots), lambda i: (half, 0)),
            pl.BlockSpec((slots, width), lambda i: (0, 0)),
        ],
        out_specs=pl.BlockSpec((tokens // 2, width), lambda i: (0, 0)),
        compiler_params=pltpu.CompilerParams(vmem_limit_bytes=32 * 2**20),
        cost_estimate=pl.CostEstimate(
            flops=tokens * slots * width, bytes_accessed=5 * 10**6, transcendentals=0
        ),
        name="merge_rows",
    )(merge, rows)


def swap_cores(array):
    return lax.ppermute(array, "local", [(i, i ^ 1) for i in range(LOCAL)])


def across_chips(array):
    groups = [[side + 2 * chip for chip in range(LOCAL // 2)] for side in range(2)]
    return lax.all_to_all(
        array, "local", split_axis=0, concat_axis=0, tiled=True, axis_index_groups=groups
    )


def along_row(array):
    nodes = lax.axis_size("node")
    groups = [[row + z for z in range(NODE_ROW)] for row in range(0, nodes, NODE_ROW)]
    return lax.all_to_all(
        array, "node", split_axis=0, concat_axis=0, tiled=True, axis_index_groups=groups
    )


def across_rows(array):
    nodes = lax.axis_size("node")
    groups = [[row + z for row in range(0, nodes, NODE_ROW)] for z in range(NODE_ROW)]
    return lax.all_to_all(
        array, "node", split_axis=0, concat_axis=0, tiled=True, axis_index_groups=groups
    )


def across_nodes(array):
    return lax.all_to_all(array, "node", split_axis=0, concat_axis=0, tiled=True)


def local(
    hidden_in, queries, key_vectors, values, out_gate, log_decay, write_rate, norm_gain,
    out_weight, post_gain, expert_index, route_weight, expert_gate_up, expert_down,
):
    node_count = lax.axis_size("node")
    local_index = lax.axis_index("local")
    side = local_index % 2
    tokens, top = expert_index.shape
    chips = LOCAL // 2
    share = tokens // LOCAL
    width = hidden_in.shape[1]
    capacity = 6 * tokens * top // (5 * node_count * LOCAL)
    side_array = side.astype(jnp.int32).reshape(1)

    def by_side(array):
        split = array.T.reshape(top, chips, 2, share)
        split = jnp.where(side == 0, split, split[:, :, ::-1])
        return split.transpose(0, 2, 1, 3).reshape(top, tokens)

    pick, merge = routing(
        local_index.astype(jnp.int32).reshape(1), by_side(expert_index), by_side(route_weight),
        node_count, capacity,
    )

    payload, cum, inner, value_rows, starts = shard_maps(key_vectors, values, log_decay.T, write_rate.T)
    maps = along_row(payload)
    core, reach = block_reads(queries, key_vectors, cum, inner, value_rows, starts)
    maps, core, reach, pick, merge = lax.optimization_barrier((maps, core, reach, pick, merge))
    totals = across_rows(row_total(maps, node_count // NODE_ROW))
    row = (lax.axis_index("node") // NODE_ROW).astype(jnp.int32).reshape(1)
    carried = along_row(shard_starts(row, totals, maps)).reshape(HEADS * DV, DK)
    own_half, other_part = gated_part(
        side_array, core, reach, carried, out_gate, norm_gain.reshape(1, DV), out_weight
    )
    given_part = swap_cores(other_part)
    kept_part = project(own_half, out_weight)
    partial = (kept_part.astype(f32) + given_part.astype(f32)).astype(bf16)
    parts = across_chips(partial.reshape(chips, share, width))
    hidden_state, normed = residual(parts, hidden_in, post_gain.reshape(1, width))
    own_rows = across_chips(normed).reshape(chips * share, width)
    rows = pick_rows(pick, own_rows, swap_cores(own_rows)).reshape(node_count, capacity, width)
    rows = across_nodes(rows).reshape(node_count * capacity, width)
    gate_up = jnp.dot(rows, expert_gate_up[0], preferred_element_type=f32)
    half_width = gate_up.shape[1] // 2
    hidden_rows = (jax.nn.silu(gate_up[:, :half_width]) * gate_up[:, half_width:]).astype(bf16)
    results = jnp.dot(hidden_rows, expert_down[0], preferred_element_type=f32).astype(bf16)
    returned = across_nodes(results.reshape(node_count, capacity, width)).reshape(
        node_count * capacity, width
    )
    given = swap_cores(merge_rows(merge, 1, returned))
    kept = merge_rows(merge, 0, returned)
    summed = (kept.astype(f32) + given.astype(f32)).astype(bf16)
    arrived = across_chips(summed.reshape(chips, share, width))
    return (hidden_state + jnp.sum(arrived.astype(f32), axis=0)).astype(bf16)


def solution(mesh):
    return jax.shard_map(
        local,
        mesh=mesh,
        in_specs=(
            P(("node", "local"), None),
            P("node", "local"),
            P("node", "local"),
            P("node", "local"),
            P("node", "local"),
            P("node", "local"),
            P("node", "local"),
            P(),
            P("local", None),
            P(),
            P("node", None),
            P("node", None),
            P(("node", "local"), None, None),
            P(("node", "local"), None, None),
        ),
        out_specs=P(("node", "local"), None),
        check_vma=False,
    )
```

```python
import jax
import jax.numpy as jnp
from jax import lax
from jax.experimental import pallas as pl
from jax.experimental.pallas import tpu as pltpu
from jax.sharding import PartitionSpec as P

DK = 128
DV = 128
HEADS = 4
BLOCK = 64
STACK = HEADS * BLOCK
SPLIT = 2
NODE_ROW = 8
LOCAL = 8

f32 = jnp.float32
bf16 = jnp.bfloat16


def mm(a, b):
    return jnp.dot(a.astype(bf16), b.astype(bf16), preferred_element_type=f32)


def mm_t(a, b):
    return lax.dot_general(
        a.astype(bf16), b.astype(bf16), (((1,), (1,)), ((), ())), preferred_element_type=f32
    )


def t_mm(a, b):
    return lax.dot_general(
        a.astype(bf16), b.astype(bf16), (((0,), (0,)), ((), ())), preferred_element_type=f32
    )


def stack_rows(pieces):
    return jnp.concatenate(pieces, axis=0)


def head_column(columns):
    return stack_rows([columns[:, h : h + 1] for h in range(HEADS)])


def unit_scale(rows):
    wide = rows.astype(f32)
    return lax.rsqrt(jnp.sum(wide * wide, axis=-1, keepdims=True) + 1e-06)


def stacked_keys(key_ref, rows):
    keys = key_ref[rows, :]
    pair = [keys[:, :DK], keys[:, DK:]]
    scales = [unit_scale(p) for p in pair]
    return (
        stack_rows([pair[0], pair[0], pair[1], pair[1]]),
        stack_rows([scales[0], scales[0], scales[1], scales[1]]),
    )


def grid_places():
    row = lax.broadcasted_iota(jnp.int32, (STACK, STACK), 0)
    col = lax.broadcasted_iota(jnp.int32, (STACK, STACK), 1)
    return row, col, (row // BLOCK) == (col // BLOCK)


def as_row(column, row, col):
    return jnp.sum(jnp.where(row == col, column, 0.0), axis=0, keepdims=True)


def maps_kernel(
    key_ref, value_ref, decay_ref, rate_ref,
    payload_ref, cum_ref, inner_ref, values_ref, starts_ref,
    rate_s, tail_s, state_s, values_s,
):
    tokens = key_ref.shape[0]
    blocks = tokens // BLOCK
    lane = lax.broadcasted_iota(jnp.int32, (HEADS, tokens), 1) % BLOCK
    total = decay_ref[...]
    step = 1
    while step < BLOCK:
        total = total + jnp.where(lane >= step, pltpu.roll(total, step, 1), 0.0)
        step *= 2
    cum_ref[...] = total.T
    rate_s[...] = rate_ref[...].T

    def one_block(b):
        rows = pl.ds(b * BLOCK, BLOCK)
        row, col, same = grid_places()
        keys, scale = stacked_keys(key_ref, rows)
        cum = cum_ref[rows, :]
        cum_col = head_column(cum)
        rate_col = head_column(rate_s[rows, :])
        last_col = stack_rows(
            [jnp.broadcast_to(cum[BLOCK - 1 : BLOCK, h : h + 1], (BLOCK, 1)) for h in range(HEADS)]
        )
        strict = jnp.logical_and(same, row > col)
        past = jnp.exp(cum_col) * scale
        onward = as_row(jnp.exp(-cum_col) * scale, row, col)
        power = jnp.where(strict, mm_t(keys, keys) * ((-rate_col * past) * onward), 0.0)
        raw = value_ref[rows, :]
        wide = keys.astype(f32)
        answer = jnp.concatenate(
            [
                rate_col * stack_rows([raw[:, h * DV : (h + 1) * DV] for h in range(HEADS)]).astype(f32),
                (rate_col * past) * wide,
            ],
            axis=1,
        )
        return rows, power, answer, (jnp.exp(last_col - cum_col) * scale) * wide

    def finish(b, answer, tail):
        values_s[b] = answer[:, :DV]
        values_ref[b] = answer[:, :DV].astype(bf16)
        inner_ref[b] = answer[:, DV:].astype(bf16)
        tail_s[b] = tail.astype(bf16)

    for first in range(0, blocks, 4):
        group = range(first, first + 4)
        made = [one_block(b) for b in group]
        powers = [m[1] for m in made]
        answers = [m[2] for m in made]
        reach = 1
        while reach < BLOCK:
            answers = [a + mm(p, a) for p, a in zip(powers, answers)]
            reach *= 2
            if reach < BLOCK:
                powers = [mm(p, p) for p in powers]
        for b, a, m in zip(group, answers, made):
            finish(b, a, m[3])

    place = lax.broadcasted_iota(jnp.int32, (DK, DV + DK), 0)
    lane_place = lax.broadcasted_iota(jnp.int32, (DK, DV + DK), 1)
    for h in range(HEADS):
        state_s[h] = jnp.where(lane_place == place + DV, 1.0, 0.0)

    def advance(b, carry):
        last = cum_ref[pl.ds(b * BLOCK + BLOCK - 1, 1), :]
        parts = [slice(h * BLOCK, (h + 1) * BLOCK) for h in range(HEADS)]
        states = [state_s[h] for h in range(HEADS)]
        rounded = [state.astype(bf16) for state in states]
        changes = [mm(inner_ref[b, part, :], now) for part, now in zip(parts, rounded)]
        given = [
            jnp.concatenate([values_s[b, part, :] - change[:, :DV], -change[:, DV:]], axis=1)
            for part, change in zip(parts, changes)
        ]
        added = [t_mm(tail_s[b, part, :], rows) for part, rows in zip(parts, given)]
        for h in range(HEADS):
            starts_ref[b, h] = rounded[h]
            state_s[h] = jnp.exp(last[:, h : h + 1]) * states[h] + added[h]
        return carry

    lax.fori_loop(0, blocks, advance, 0, unroll=True)
    share = DV // SPLIT
    for h in range(HEADS):
        state = state_s[h]
        inject = state[:, :DV].T.astype(bf16)
        move = state[:, DV:].T.astype(bf16)
        for s in range(SPLIT):
            payload_ref[h * SPLIT + s, :DK, :] = move
            payload_ref[h * SPLIT + s, DK:, :] = inject[s * share : (s + 1) * share, :]


def shard_maps(keys, values, decay, rate):
    tokens = keys.shape[0]
    blocks = tokens // BLOCK
    return pl.pallas_call(
        maps_kernel,
        out_shape=(
            jax.ShapeDtypeStruct((HEADS * SPLIT, DK + DV // SPLIT, DK), bf16),
            jax.ShapeDtypeStruct((tokens, HEADS), f32),
            jax.ShapeDtypeStruct((blocks, STACK, DK), bf16),
            jax.ShapeDtypeStruct((blocks, STACK, DV), bf16),
            jax.ShapeDtypeStruct((blocks, HEADS, DK, DV + DK), bf16),
        ),
        scratch_shapes=[
            pltpu.VMEM((tokens, HEADS), f32),
            pltpu.VMEM((blocks, STACK, DK), bf16),
            pltpu.VMEM((HEADS, DK, DV + DK), f32),
            pltpu.VMEM((blocks, STACK, DV), f32),
        ],
        compiler_params=pltpu.CompilerParams(vmem_limit_bytes=60 * 2**20),
        name="shard_maps",
    )(keys, values, decay, rate)


def reads_kernel(query_ref, key_ref, cum_ref, inner_ref, values_ref, starts_ref, core_ref, reach_ref):
    blocks = query_ref.shape[0] // BLOCK

    def one_block(b):
        rows = pl.ds(b * BLOCK, BLOCK)
        row, col, same = grid_places()
        keys, scale = stacked_keys(key_ref, rows)
        queries, query_scale = stacked_keys(query_ref, rows)
        query_scale = query_scale * DK ** (-0.5)
        cum_col = head_column(cum_ref[rows, :])
        inclusive = jnp.logical_and(same, row >= col)
        past = jnp.exp(cum_col) * query_scale
        onward = as_row(jnp.exp(-cum_col) * scale, row, col)
        attention = jnp.where(inclusive, mm_t(queries, keys) * (past * onward), 0.0)
        both = mm(attention, jnp.concatenate([values_ref[b], inner_ref[b]], axis=1))
        emitter = (past * queries.astype(f32) - both[:, DV:]).astype(bf16)
        for h in range(HEADS):
            part = slice(h * BLOCK, (h + 1) * BLOCK)
            read = mm(emitter[part, :], starts_ref[b, h])
            core_ref[rows, h * DV : (h + 1) * DV] = both[part, :DV] + read[:, :DV]
            reach_ref[rows, h * DK : (h + 1) * DK] = read[:, DV:].astype(bf16)

    for b in range(blocks):
        one_block(b)


def block_reads(queries, keys, cum, inner, values, starts):
    tokens = keys.shape[0]
    return pl.pallas_call(
        reads_kernel,
        out_shape=(
            jax.ShapeDtypeStruct((tokens, HEADS * DV), f32),
            jax.ShapeDtypeStruct((tokens, HEADS * DK), bf16),
        ),
        compiler_params=pltpu.CompilerParams(vmem_limit_bytes=60 * 2**20),
        cost_estimate=pl.CostEstimate(flops=2 * 10**9, bytes_accessed=8 * 10**6, transcendentals=10**6),
        name="block_reads",
    )(queries, keys, cum, inner, values, starts)


def step(state, move):
    rows = state.shape[0]
    high = state.astype(bf16)
    low = (state - high.astype(f32)).astype(bf16)
    moved = jnp.dot(jnp.concatenate([high, low], axis=0), move, preferred_element_type=f32)
    return moved[:rows] + moved[rows:]


def row_total_kernel(maps_ref, total_ref):
    total = maps_ref[0].astype(f32)
    for k in range(1, maps_ref.shape[0]):
        moved = step(total, maps_ref[k, :DK, :])
        total = jnp.concatenate([moved[:DK], moved[DK:] + maps_ref[k, DK:, :].astype(f32)], axis=0)
    for copy in range(total_ref.shape[0]):
        total_ref[copy] = total.astype(bf16)


def row_total(maps, rows):
    return pl.pallas_call(
        row_total_kernel,
        out_shape=jax.ShapeDtypeStruct((rows,) + maps.shape[1:], bf16),
        compiler_params=pltpu.CompilerParams(vmem_limit_bytes=32 * 2**20),
        name="row_total",
    )(maps)


def starts_kernel(row_ref, totals_ref, maps_ref, start_ref):
    def apply(state, ref, k):
        return step(state, ref[k, :DK, :]) + ref[k, DK:, :].astype(f32)

    state = jnp.zeros(start_ref.shape[1:], f32)
    for k in range(totals_ref.shape[0] - 1):
        state = jnp.where(k < row_ref[0], apply(state, totals_ref, k), state)
    for k in range(maps_ref.shape[0]):
        start_ref[k] = state.astype(bf16)
        if k + 1 < maps_ref.shape[0]:
            state = apply(state, maps_ref, k)


def shard_starts(row, totals, maps):
    vmem = pl.BlockSpec(memory_space=pltpu.VMEM)
    return pl.pallas_call(
        starts_kernel,
        out_shape=jax.ShapeDtypeStruct((maps.shape[0], maps.shape[1] - DK, DK), bf16),
        in_specs=[pl.BlockSpec(memory_space=pltpu.SMEM), vmem, vmem],
        out_specs=vmem,
        compiler_params=pltpu.CompilerParams(vmem_limit_bytes=32 * 2**20),
        name="shard_starts",
    )(row, totals, maps)


def gated_kernel(
    core_side, core_ref, reach_ref, start_ref, gate_ref, gain_ref, weight_hbm,
    own_ref, part_ref, gated_s, other_s, weight_s, arrival,
):
    fetch = pltpu.make_async_copy(weight_hbm, weight_s, arrival)
    fetch.start()
    share = core_ref.shape[0] // LOCAL
    lanes = [slice(h * DV, (h + 1) * DV) for h in range(HEADS)]
    reads = [mm_t(reach_ref[:, lane], start_ref[lane, :]) for lane in lanes]
    for lane, read in zip(lanes, reads):
        core = core_ref[:, lane] + read
        core = core * lax.rsqrt(jnp.mean(core * core, axis=-1, keepdims=True) + 1e-06)
        gate = gate_ref[:, lane].astype(f32)
        gated_s[:, lane] = (core * gain_ref[...] * (gate / (1.0 + jnp.exp(-gate)))).astype(bf16)
    side = core_side[0]
    for chip in range(LOCAL // 2):
        for ref, parity in ((own_ref, side), (other_s, 1 - side)):
            first = pl.multiple_of((2 * chip + parity) * share, share)
            ref[chip * share : (chip + 1) * share, :] = gated_s[pl.ds(first, share), :]
    fetch.wait()
    part_ref[...] = mm(other_s[...], weight_s[...]).astype(bf16)


def gated_part(side, core, reach, starts, gate, gain, weight):
    tokens, depth = core.shape
    half = tokens // 2
    vmem = pl.BlockSpec(memory_space=pltpu.VMEM)
    return pl.pallas_call(
        gated_kernel,
        out_shape=(
            jax.ShapeDtypeStruct((half, depth), bf16),
            jax.ShapeDtypeStruct((half, weight.shape[1]), bf16),
        ),
        in_specs=[pl.BlockSpec(memory_space=pltpu.SMEM)]
        + [vmem] * 5
        + [pl.BlockSpec(memory_space=pl.ANY)],
        out_specs=(vmem, vmem),
        scratch_shapes=[
            pltpu.VMEM((tokens, depth), bf16),
            pltpu.VMEM((half, depth), bf16),
            pltpu.VMEM(weight.shape, bf16),
            pltpu.SemaphoreType.DMA,
        ],
        compiler_params=pltpu.CompilerParams(vmem_limit_bytes=60 * 2**20),
        name="gated_part",
    )(side, core, reach, starts, gate, gain, weight)


def project_kernel(rows_ref, weight_ref, out_ref):
    out_ref[...] = mm(rows_ref[...], weight_ref[...]).astype(bf16)


def project(rows, weight):
    return pl.pallas_call(
        project_kernel,
        out_shape=jax.ShapeDtypeStruct((rows.shape[0], weight.shape[1]), bf16),
        compiler_params=pltpu.CompilerParams(vmem_limit_bytes=32 * 2**20),
        cost_estimate=pl.CostEstimate(
            flops=2 * rows.size * weight.shape[1], bytes_accessed=4 * 10**6, transcendentals=0
        ),
        name="project",
    )(rows, weight)


def residual_kernel(parts_ref, hidden_ref, gain_ref, state_ref, normed_ref):
    state = hidden_ref[...].astype(f32)
    for part in range(parts_ref.shape[0]):
        state = state + parts_ref[part].astype(f32)
    state_ref[...] = state
    normed = state * lax.rsqrt(jnp.mean(state * state, axis=-1, keepdims=True) + 1e-06) * gain_ref[...]
    for copy in range(normed_ref.shape[0]):
        normed_ref[copy] = normed.astype(bf16)


def residual(parts, hidden, gain):
    return pl.pallas_call(
        residual_kernel,
        out_shape=(
            jax.ShapeDtypeStruct(hidden.shape, f32),
            jax.ShapeDtypeStruct(parts.shape, bf16),
        ),
        compiler_params=pltpu.CompilerParams(vmem_limit_bytes=32 * 2**20),
        name="residual",
    )(parts, hidden, gain)


def routing_kernel(capacity, place_ref, index_ref, weight_ref, pick_ref, merge_ref, slot_s, share_s, wide_s):
    top, tokens = index_ref.shape
    groups = slot_s.shape[0]
    ids = lax.broadcasted_iota(jnp.int32, (groups, 1), 0) * LOCAL + place_ref[0]
    member = jnp.zeros((groups, tokens), f32)
    share = jnp.zeros((groups, tokens), f32)
    for j in range(top):
        hit = index_ref[j : j + 1, :] == ids
        member = jnp.where(hit, 1.0, member)
        share = jnp.where(hit, weight_ref[j : j + 1, :], share)
    earlier = lax.broadcasted_iota(jnp.int32, (tokens, tokens), 0) < lax.broadcasted_iota(
        jnp.int32, (tokens, tokens), 1
    )
    rank = mm(member, jnp.where(earlier, 1.0, 0.0))
    slot_s[...] = jnp.where(member > 0.0, rank, -1.0)
    share_s[...] = share
    several = 4
    span = several * capacity
    for i in range(groups // several):
        slot = slot_s[i * several : (i + 1) * several, :]
        part = share_s[i * several : (i + 1) * several, :]
        place = lax.broadcasted_iota(jnp.int32, (several, capacity, tokens), 1).astype(f32)
        hit = slot[:, None, :] == place
        pick_ref[i * span : (i + 1) * span, :] = (
            jnp.where(hit, 1.0, 0.0).reshape(span, tokens).astype(bf16)
        )
        wide_s[i * span : (i + 1) * span, :] = jnp.where(hit, part[:, None, :], 0.0).reshape(
            span, tokens
        )
    for i in range(groups * capacity // 128):
        merge_ref[:, i * 128 : (i + 1) * 128] = wide_s[i * 128 : (i + 1) * 128, :].T.astype(bf16)


def routing(place, index, weight, groups, capacity):
    top, tokens = index.shape
    slots = groups * capacity
    vmem = pl.BlockSpec(memory_space=pltpu.VMEM)
    return pl.pallas_call(
        lambda *refs: routing_kernel(capacity, *refs),
        out_shape=(
            jax.ShapeDtypeStruct((slots, tokens), bf16),
            jax.ShapeDtypeStruct((tokens, slots), bf16),
        ),
        in_specs=[pl.BlockSpec(memory_space=pltpu.SMEM), vmem, vmem],
        out_specs=(vmem, vmem),
        scratch_shapes=[
            pltpu.VMEM((groups, tokens), f32),
            pltpu.VMEM((groups, tokens), f32),
            pltpu.VMEM((slots, tokens), f32),
        ],
        compiler_params=pltpu.CompilerParams(vmem_limit_bytes=32 * 2**20),
        cost_estimate=pl.CostEstimate(flops=3 * 10**9, bytes_accessed=6 * 10**6, transcendentals=0),
        name="routing",
    )(place, index, weight)


def pick_kernel(pick_ref, rows_ref, out_ref):
    out_ref[...] = mm(pick_ref[...], rows_ref[...]).astype(bf16)


def pick_more_kernel(pick_ref, rows_ref, found_ref, out_ref):
    out_ref[...] = (mm(pick_ref[...], rows_ref[...]) + found_ref[...].astype(f32)).astype(bf16)


def pick_rows(pick, half, rows, *found):
    slots = pick.shape[0]
    tokens, width = rows.shape
    tile = width // 2
    out_spec = pl.BlockSpec((slots, tile), lambda i: (0, i))
    return pl.pallas_call(
        pick_more_kernel if found else pick_kernel,
        out_shape=jax.ShapeDtypeStruct((slots, width), bf16),
        grid=(width // tile,),
        in_specs=[
            pl.BlockSpec((slots, tokens), lambda i: (0, half)),
            pl.BlockSpec((tokens, tile), lambda i: (0, i)),
        ]
        + [out_spec] * len(found),
        out_specs=out_spec,
        compiler_params=pltpu.CompilerParams(vmem_limit_bytes=32 * 2**20),
        cost_estimate=pl.CostEstimate(
            flops=2 * slots * tokens * width, bytes_accessed=5 * 10**6, transcendentals=0
        ),
        name="pick_rows",
    )(pick, rows, *found)


def merge_kernel(merge_ref, rows_ref, out_ref):
    out_ref[...] = mm(merge_ref[...], rows_ref[...]).astype(bf16)


def merge_rows(merge, half, rows):
    tokens, slots = merge.shape
    width = rows.shape[1]
    return pl.pallas_call(
        merge_kernel,
        out_shape=jax.ShapeDtypeStruct((tokens // 2, width), bf16),
        grid=(1,),
        in_specs=[
            pl.BlockSpec((tokens // 2, slots), lambda i: (half, 0)),
            pl.BlockSpec((slots, width), lambda i: (0, 0)),
        ],
        out_specs=pl.BlockSpec((tokens // 2, width), lambda i: (0, 0)),
        compiler_params=pltpu.CompilerParams(vmem_limit_bytes=32 * 2**20),
        cost_estimate=pl.CostEstimate(
            flops=tokens * slots * width, bytes_accessed=5 * 10**6, transcendentals=0
        ),
        name="merge_rows",
    )(merge, rows)


def swap_cores(array):
    return lax.ppermute(array, "local", [(i, i ^ 1) for i in range(LOCAL)])


def across_chips(array):
    groups = [[side + 2 * chip for chip in range(LOCAL // 2)] for side in range(2)]
    return lax.all_to_all(
        array, "local", split_axis=0, concat_axis=0, tiled=True, axis_index_groups=groups
    )


def along_row(array):
    nodes = lax.axis_size("node")
    groups = [[row + z for z in range(NODE_ROW)] for row in range(0, nodes, NODE_ROW)]
    return lax.all_to_all(
        array, "node", split_axis=0, concat_axis=0, tiled=True, axis_index_groups=groups
    )


def across_rows(array):
    nodes = lax.axis_size("node")
    groups = [[row + z for row in range(0, nodes, NODE_ROW)] for z in range(NODE_ROW)]
    return lax.all_to_all(
        array, "node", split_axis=0, concat_axis=0, tiled=True, axis_index_groups=groups
    )


def across_nodes(array):
    return lax.all_to_all(array, "node", split_axis=0, concat_axis=0, tiled=True)


def local(
    hidden_in, queries, key_vectors, values, out_gate, log_decay, write_rate, norm_gain,
    out_weight, post_gain, expert_index, route_weight, expert_gate_up, expert_down,
):
    node_count = lax.axis_size("node")
    local_index = lax.axis_index("local")
    side = local_index % 2
    tokens, top = expert_index.shape
    chips = LOCAL // 2
    share = tokens // LOCAL
    width = hidden_in.shape[1]
    capacity = 6 * tokens * top // (5 * node_count * LOCAL)
    side_array = side.astype(jnp.int32).reshape(1)

    def by_side(array):
        split = array.T.reshape(top, chips, 2, share)
        split = jnp.where(side == 0, split, split[:, :, ::-1])
        return split.transpose(0, 2, 1, 3).reshape(top, tokens)

    pick, merge = routing(
        local_index.astype(jnp.int32).reshape(1), by_side(expert_index), by_side(route_weight),
        node_count, capacity,
    )

    payload, cum, inner, value_rows, starts = shard_maps(key_vectors, values, log_decay.T, write_rate.T)
    maps = along_row(payload)
    core, reach = block_reads(queries, key_vectors, cum, inner, value_rows, starts)
    maps, core, reach, pick, merge = lax.optimization_barrier((maps, core, reach, pick, merge))
    totals = across_rows(row_total(maps, node_count // NODE_ROW))
    row = (lax.axis_index("node") // NODE_ROW).astype(jnp.int32).reshape(1)
    carried = along_row(shard_starts(row, totals, maps)).reshape(HEADS * DV, DK)
    own_half, other_part = gated_part(
        side_array, core, reach, carried, out_gate, norm_gain.reshape(1, DV), out_weight
    )
    given_part = swap_cores(other_part)
    kept_part = project(own_half, out_weight)
    partial = (kept_part.astype(f32) + given_part.astype(f32)).astype(bf16)
    parts = across_chips(partial.reshape(chips, share, width))
    hidden_state, normed = residual(parts, hidden_in, post_gain.reshape(1, width))
    own_rows = across_chips(normed).reshape(chips * share, width)
    other_rows = swap_cores(own_rows)
    found = pick_rows(pick, 0, own_rows)
    rows = pick_rows(pick, 1, other_rows, found).reshape(node_count, capacity, width)
    rows = across_nodes(rows).reshape(node_count * capacity, width)
    gate_up = jnp.dot(rows, expert_gate_up[0], preferred_element_type=f32)
    half_width = gate_up.shape[1] // 2
    hidden_rows = (jax.nn.silu(gate_up[:, :half_width]) * gate_up[:, half_width:]).astype(bf16)
    results = jnp.dot(hidden_rows, expert_down[0], preferred_element_type=f32).astype(bf16)
    returned = across_nodes(results.reshape(node_count, capacity, width)).reshape(
        node_count * capacity, width
    )
    given = swap_cores(merge_rows(merge, 1, returned))
    kept = merge_rows(merge, 0, returned)
    summed = (kept.astype(f32) + given.astype(f32)).astype(bf16)
    arrived = across_chips(summed.reshape(chips, share, width))
    return (hidden_state + jnp.sum(arrived.astype(f32), axis=0)).astype(bf16)


def solution(mesh):
    return jax.shard_map(
        local,
        mesh=mesh,
        in_specs=(
            P(("node", "local"), None),
            P("node", "local"),
            P("node", "local"),
            P("node", "local"),
            P("node", "local"),
            P("node", "local"),
            P("node", "local"),
            P(),
            P("local", None),
            P(),
            P("node", None),
            P("node", None),
            P(("node", "local"), None, None),
            P(("node", "local"), None, None),
        ),
        out_specs=P(("node", "local"), None),
        check_vma=False,
    )
```

```python
import jax
import jax.numpy as jnp
from jax import lax
from jax.experimental import pallas as pl
from jax.experimental.pallas import tpu as pltpu
from jax.sharding import PartitionSpec as P

DK = 128
DV = 128
HEADS = 4
BLOCK = 64
STACK = HEADS * BLOCK
SPLIT = 2
NODE_ROW = 8
LOCAL = 8

f32 = jnp.float32
bf16 = jnp.bfloat16


def mm(a, b):
    return jnp.dot(a.astype(bf16), b.astype(bf16), preferred_element_type=f32)


def mm_t(a, b):
    return lax.dot_general(
        a.astype(bf16), b.astype(bf16), (((1,), (1,)), ((), ())), preferred_element_type=f32
    )


def t_mm(a, b):
    return lax.dot_general(
        a.astype(bf16), b.astype(bf16), (((0,), (0,)), ((), ())), preferred_element_type=f32
    )


def stack_rows(pieces):
    return jnp.concatenate(pieces, axis=0)


def head_column(columns):
    return stack_rows([columns[:, h : h + 1] for h in range(HEADS)])


def unit_scale(rows):
    wide = rows.astype(f32)
    return lax.rsqrt(jnp.sum(wide * wide, axis=-1, keepdims=True) + 1e-06)


def stacked_keys(key_ref, rows):
    keys = key_ref[rows, :]
    pair = [keys[:, :DK], keys[:, DK:]]
    scales = [unit_scale(p) for p in pair]
    return (
        stack_rows([pair[0], pair[0], pair[1], pair[1]]),
        stack_rows([scales[0], scales[0], scales[1], scales[1]]),
    )


def grid_places():
    row = lax.broadcasted_iota(jnp.int32, (STACK, STACK), 0)
    col = lax.broadcasted_iota(jnp.int32, (STACK, STACK), 1)
    return row, col, (row // BLOCK) == (col // BLOCK)


def as_row(column, row, col):
    return jnp.sum(jnp.where(row == col, column, 0.0), axis=0, keepdims=True)


def maps_kernel(
    key_ref, value_ref, decay_ref, rate_ref,
    payload_ref, cum_ref, inner_ref, values_ref, starts_ref,
    rate_s, tail_s, state_s, values_s,
):
    tokens = key_ref.shape[0]
    blocks = tokens // BLOCK
    lane = lax.broadcasted_iota(jnp.int32, (HEADS, tokens), 1) % BLOCK
    total = decay_ref[...]
    step = 1
    while step < BLOCK:
        total = total + jnp.where(lane >= step, pltpu.roll(total, step, 1), 0.0)
        step *= 2
    cum_ref[...] = total.T
    rate_s[...] = rate_ref[...].T

    def one_block(b):
        rows = pl.ds(b * BLOCK, BLOCK)
        row, col, same = grid_places()
        keys, scale = stacked_keys(key_ref, rows)
        cum = cum_ref[rows, :]
        cum_col = head_column(cum)
        rate_col = head_column(rate_s[rows, :])
        last_col = stack_rows(
            [jnp.broadcast_to(cum[BLOCK - 1 : BLOCK, h : h + 1], (BLOCK, 1)) for h in range(HEADS)]
        )
        strict = jnp.logical_and(same, row > col)
        past = jnp.exp(cum_col) * scale
        onward = as_row(jnp.exp(-cum_col) * scale, row, col)
        power = jnp.where(strict, mm_t(keys, keys) * ((-rate_col * past) * onward), 0.0)
        raw = value_ref[rows, :]
        wide = keys.astype(f32)
        answer = jnp.concatenate(
            [
                rate_col * stack_rows([raw[:, h * DV : (h + 1) * DV] for h in range(HEADS)]).astype(f32),
                (rate_col * past) * wide,
            ],
            axis=1,
        )
        return rows, power, answer, (jnp.exp(last_col - cum_col) * scale) * wide

    def finish(b, answer, tail):
        values_s[b] = answer[:, :DV]
        values_ref[b] = answer[:, :DV].astype(bf16)
        inner_ref[b] = answer[:, DV:].astype(bf16)
        tail_s[b] = tail.astype(bf16)

    for first in range(0, blocks, 4):
        group = range(first, first + 4)
        made = [one_block(b) for b in group]
        powers = [m[1] for m in made]
        answers = [m[2] for m in made]
        reach = 1
        while reach < BLOCK:
            answers = [a + mm(p, a) for p, a in zip(powers, answers)]
            reach *= 2
            if reach < BLOCK:
                powers = [mm(p, p) for p in powers]
        for b, a, m in zip(group, answers, made):
            finish(b, a, m[3])

    place = lax.broadcasted_iota(jnp.int32, (DK, DV + DK), 0)
    lane_place = lax.broadcasted_iota(jnp.int32, (DK, DV + DK), 1)
    for h in range(HEADS):
        state_s[h] = jnp.where(lane_place == place + DV, 1.0, 0.0)

    def advance(b, carry):
        last = cum_ref[pl.ds(b * BLOCK + BLOCK - 1, 1), :]
        parts = [slice(h * BLOCK, (h + 1) * BLOCK) for h in range(HEADS)]
        states = [state_s[h] for h in range(HEADS)]
        rounded = [state.astype(bf16) for state in states]
        changes = [mm(inner_ref[b, part, :], now) for part, now in zip(parts, rounded)]
        given = [
            jnp.concatenate([values_s[b, part, :] - change[:, :DV], -change[:, DV:]], axis=1)
            for part, change in zip(parts, changes)
        ]
        added = [t_mm(tail_s[b, part, :], rows) for part, rows in zip(parts, given)]
        for h in range(HEADS):
            starts_ref[b, h] = rounded[h]
            state_s[h] = jnp.exp(last[:, h : h + 1]) * states[h] + added[h]
        return carry

    lax.fori_loop(0, blocks, advance, 0, unroll=True)
    share = DV // SPLIT
    for h in range(HEADS):
        state = state_s[h]
        inject = state[:, :DV].T.astype(bf16)
        move = state[:, DV:].T.astype(bf16)
        for s in range(SPLIT):
            payload_ref[h * SPLIT + s, :DK, :] = move
            payload_ref[h * SPLIT + s, DK:, :] = inject[s * share : (s + 1) * share, :]


def shard_maps(keys, values, decay, rate):
    tokens = keys.shape[0]
    blocks = tokens // BLOCK
    return pl.pallas_call(
        maps_kernel,
        out_shape=(
            jax.ShapeDtypeStruct((HEADS * SPLIT, DK + DV // SPLIT, DK), bf16),
            jax.ShapeDtypeStruct((tokens, HEADS), f32),
            jax.ShapeDtypeStruct((blocks, STACK, DK), bf16),
            jax.ShapeDtypeStruct((blocks, STACK, DV), bf16),
            jax.ShapeDtypeStruct((blocks, HEADS, DK, DV + DK), bf16),
        ),
        scratch_shapes=[
            pltpu.VMEM((tokens, HEADS), f32),
            pltpu.VMEM((blocks, STACK, DK), bf16),
            pltpu.VMEM((HEADS, DK, DV + DK), f32),
            pltpu.VMEM((blocks, STACK, DV), f32),
        ],
        compiler_params=pltpu.CompilerParams(vmem_limit_bytes=60 * 2**20),
        name="shard_maps",
    )(keys, values, decay, rate)


def reads_kernel(query_ref, key_ref, cum_ref, inner_ref, values_ref, starts_ref, core_ref, reach_ref):
    blocks = query_ref.shape[0] // BLOCK

    def one_block(b):
        rows = pl.ds(b * BLOCK, BLOCK)
        row, col, same = grid_places()
        keys, scale = stacked_keys(key_ref, rows)
        queries, query_scale = stacked_keys(query_ref, rows)
        query_scale = query_scale * DK ** (-0.5)
        cum_col = head_column(cum_ref[rows, :])
        inclusive = jnp.logical_and(same, row >= col)
        past = jnp.exp(cum_col) * query_scale
        onward = as_row(jnp.exp(-cum_col) * scale, row, col)
        attention = jnp.where(inclusive, mm_t(queries, keys) * (past * onward), 0.0)
        both = mm(attention, jnp.concatenate([values_ref[b], inner_ref[b]], axis=1))
        emitter = (past * queries.astype(f32) - both[:, DV:]).astype(bf16)
        for h in range(HEADS):
            part = slice(h * BLOCK, (h + 1) * BLOCK)
            read = mm(emitter[part, :], starts_ref[b, h])
            core_ref[rows, h * DV : (h + 1) * DV] = both[part, :DV] + read[:, :DV]
            reach_ref[rows, h * DK : (h + 1) * DK] = read[:, DV:].astype(bf16)

    for b in range(blocks):
        one_block(b)


def block_reads(queries, keys, cum, inner, values, starts):
    tokens = keys.shape[0]
    return pl.pallas_call(
        reads_kernel,
        out_shape=(
            jax.ShapeDtypeStruct((tokens, HEADS * DV), f32),
            jax.ShapeDtypeStruct((tokens, HEADS * DK), bf16),
        ),
        compiler_params=pltpu.CompilerParams(vmem_limit_bytes=60 * 2**20),
        cost_estimate=pl.CostEstimate(flops=2 * 10**9, bytes_accessed=8 * 10**6, transcendentals=10**6),
        name="block_reads",
    )(queries, keys, cum, inner, values, starts)


def step(state, move):
    rows = state.shape[0]
    high = state.astype(bf16)
    low = (state - high.astype(f32)).astype(bf16)
    moved = jnp.dot(jnp.concatenate([high, low], axis=0), move, preferred_element_type=f32)
    return moved[:rows] + moved[rows:]


def row_total_kernel(maps_ref, total_ref):
    total = maps_ref[0].astype(f32)
    for k in range(1, maps_ref.shape[0]):
        moved = step(total, maps_ref[k, :DK, :])
        total = jnp.concatenate([moved[:DK], moved[DK:] + maps_ref[k, DK:, :].astype(f32)], axis=0)
    for copy in range(total_ref.shape[0]):
        total_ref[copy] = total.astype(bf16)


def row_total(maps, rows):
    return pl.pallas_call(
        row_total_kernel,
        out_shape=jax.ShapeDtypeStruct((rows,) + maps.shape[1:], bf16),
        compiler_params=pltpu.CompilerParams(vmem_limit_bytes=32 * 2**20),
        name="row_total",
    )(maps)


def starts_kernel(row_ref, totals_ref, maps_ref, start_ref):
    def apply(state, ref, k):
        return step(state, ref[k, :DK, :]) + ref[k, DK:, :].astype(f32)

    state = jnp.zeros(start_ref.shape[1:], f32)
    for k in range(totals_ref.shape[0] - 1):
        state = jnp.where(k < row_ref[0], apply(state, totals_ref, k), state)
    for k in range(maps_ref.shape[0]):
        start_ref[k] = state.astype(bf16)
        if k + 1 < maps_ref.shape[0]:
            state = apply(state, maps_ref, k)


def shard_starts(row, totals, maps):
    vmem = pl.BlockSpec(memory_space=pltpu.VMEM)
    return pl.pallas_call(
        starts_kernel,
        out_shape=jax.ShapeDtypeStruct((maps.shape[0], maps.shape[1] - DK, DK), bf16),
        in_specs=[pl.BlockSpec(memory_space=pltpu.SMEM), vmem, vmem],
        out_specs=vmem,
        compiler_params=pltpu.CompilerParams(vmem_limit_bytes=32 * 2**20),
        name="shard_starts",
    )(row, totals, maps)


def gated_kernel(
    core_side, core_ref, reach_ref, start_ref, gate_ref, gain_ref, weight_hbm,
    own_ref, part_ref, gated_s, other_s, weight_s, arrival,
):
    fetch = pltpu.make_async_copy(weight_hbm, weight_s, arrival)
    fetch.start()
    share = core_ref.shape[0] // LOCAL
    lanes = [slice(h * DV, (h + 1) * DV) for h in range(HEADS)]
    reads = [mm_t(reach_ref[:, lane], start_ref[lane, :]) for lane in lanes]
    for lane, read in zip(lanes, reads):
        core = core_ref[:, lane] + read
        core = core * lax.rsqrt(jnp.mean(core * core, axis=-1, keepdims=True) + 1e-06)
        gate = gate_ref[:, lane].astype(f32)
        gated_s[:, lane] = (core * gain_ref[...] * (gate / (1.0 + jnp.exp(-gate)))).astype(bf16)
    side = core_side[0]
    for chip in range(LOCAL // 2):
        for ref, parity in ((own_ref, side), (other_s, 1 - side)):
            first = pl.multiple_of((2 * chip + parity) * share, share)
            ref[chip * share : (chip + 1) * share, :] = gated_s[pl.ds(first, share), :]
    fetch.wait()
    part_ref[...] = mm(other_s[...], weight_s[...]).astype(bf16)


def gated_part(side, core, reach, starts, gate, gain, weight):
    tokens, depth = core.shape
    half = tokens // 2
    vmem = pl.BlockSpec(memory_space=pltpu.VMEM)
    return pl.pallas_call(
        gated_kernel,
        out_shape=(
            jax.ShapeDtypeStruct((half, depth), bf16),
            jax.ShapeDtypeStruct((half, weight.shape[1]), bf16),
        ),
        in_specs=[pl.BlockSpec(memory_space=pltpu.SMEM)]
        + [vmem] * 5
        + [pl.BlockSpec(memory_space=pl.ANY)],
        out_specs=(vmem, vmem),
        scratch_shapes=[
            pltpu.VMEM((tokens, depth), bf16),
            pltpu.VMEM((half, depth), bf16),
            pltpu.VMEM(weight.shape, bf16),
            pltpu.SemaphoreType.DMA,
        ],
        compiler_params=pltpu.CompilerParams(vmem_limit_bytes=60 * 2**20),
        name="gated_part",
    )(side, core, reach, starts, gate, gain, weight)


def project_kernel(rows_ref, weight_ref, given_ref, out_ref):
    out_ref[...] = (mm(rows_ref[...], weight_ref[...]) + given_ref[...].astype(f32)).astype(bf16)


def project(rows, weight, given):
    return pl.pallas_call(
        project_kernel,
        out_shape=jax.ShapeDtypeStruct((rows.shape[0], weight.shape[1]), bf16),
        compiler_params=pltpu.CompilerParams(vmem_limit_bytes=32 * 2**20),
        cost_estimate=pl.CostEstimate(
            flops=2 * rows.size * weight.shape[1], bytes_accessed=4 * 10**6, transcendentals=0
        ),
        name="project",
    )(rows, weight, given)


def residual_kernel(parts_ref, hidden_ref, gain_ref, state_ref, normed_ref):
    state = hidden_ref[...].astype(f32)
    for part in range(parts_ref.shape[0]):
        state = state + parts_ref[part].astype(f32)
    state_ref[...] = state
    normed = state * lax.rsqrt(jnp.mean(state * state, axis=-1, keepdims=True) + 1e-06) * gain_ref[...]
    for copy in range(normed_ref.shape[0]):
        normed_ref[copy] = normed.astype(bf16)


def residual(parts, hidden, gain):
    return pl.pallas_call(
        residual_kernel,
        out_shape=(
            jax.ShapeDtypeStruct(hidden.shape, f32),
            jax.ShapeDtypeStruct(parts.shape, bf16),
        ),
        compiler_params=pltpu.CompilerParams(vmem_limit_bytes=32 * 2**20),
        name="residual",
    )(parts, hidden, gain)


def finish_kernel(parts_ref, state_ref, out_ref):
    total = state_ref[...]
    for part in range(parts_ref.shape[0]):
        total = total + parts_ref[part].astype(f32)
    out_ref[...] = total.astype(bf16)


def finish(parts, state):
    return pl.pallas_call(
        finish_kernel,
        out_shape=jax.ShapeDtypeStruct(state.shape, bf16),
        compiler_params=pltpu.CompilerParams(vmem_limit_bytes=32 * 2**20),
        name="finish",
    )(parts, state)


def routing_kernel(capacity, place_ref, index_ref, weight_ref, pick_ref, merge_ref, slot_s, share_s, wide_s):
    top, tokens = index_ref.shape
    groups = slot_s.shape[0]
    ids = lax.broadcasted_iota(jnp.int32, (groups, 1), 0) * LOCAL + place_ref[0]
    member = jnp.zeros((groups, tokens), f32)
    share = jnp.zeros((groups, tokens), f32)
    for j in range(top):
        hit = index_ref[j : j + 1, :] == ids
        member = jnp.where(hit, 1.0, member)
        share = jnp.where(hit, weight_ref[j : j + 1, :], share)
    earlier = lax.broadcasted_iota(jnp.int32, (tokens, tokens), 0) < lax.broadcasted_iota(
        jnp.int32, (tokens, tokens), 1
    )
    rank = mm(member, jnp.where(earlier, 1.0, 0.0))
    slot_s[...] = jnp.where(member > 0.0, rank, -1.0)
    share_s[...] = share
    several = 4
    span = several * capacity
    for i in range(groups // several):
        slot = slot_s[i * several : (i + 1) * several, :]
        part = share_s[i * several : (i + 1) * several, :]
        place = lax.broadcasted_iota(jnp.int32, (several, capacity, tokens), 1).astype(f32)
        hit = slot[:, None, :] == place
        pick_ref[i * span : (i + 1) * span, :] = (
            jnp.where(hit, 1.0, 0.0).reshape(span, tokens).astype(bf16)
        )
        wide_s[i * span : (i + 1) * span, :] = jnp.where(hit, part[:, None, :], 0.0).reshape(
            span, tokens
        )
    for i in range(groups * capacity // 128):
        merge_ref[:, i * 128 : (i + 1) * 128] = wide_s[i * 128 : (i + 1) * 128, :].T.astype(bf16)


def routing(place, index, weight, groups, capacity):
    top, tokens = index.shape
    slots = groups * capacity
    vmem = pl.BlockSpec(memory_space=pltpu.VMEM)
    return pl.pallas_call(
        lambda *refs: routing_kernel(capacity, *refs),
        out_shape=(
            jax.ShapeDtypeStruct((slots, tokens), bf16),
            jax.ShapeDtypeStruct((tokens, slots), bf16),
        ),
        in_specs=[pl.BlockSpec(memory_space=pltpu.SMEM), vmem, vmem],
        out_specs=(vmem, vmem),
        scratch_shapes=[
            pltpu.VMEM((groups, tokens), f32),
            pltpu.VMEM((groups, tokens), f32),
            pltpu.VMEM((slots, tokens), f32),
        ],
        compiler_params=pltpu.CompilerParams(vmem_limit_bytes=32 * 2**20),
        cost_estimate=pl.CostEstimate(flops=3 * 10**9, bytes_accessed=6 * 10**6, transcendentals=0),
        name="routing",
    )(place, index, weight)


def pick_kernel(pick_ref, rows_ref, out_ref):
    out_ref[...] = mm(pick_ref[...], rows_ref[...]).astype(bf16)


def pick_more_kernel(pick_ref, rows_ref, found_ref, out_ref):
    out_ref[...] = (mm(pick_ref[...], rows_ref[...]) + found_ref[...].astype(f32)).astype(bf16)


def pick_rows(pick, half, rows, *found):
    slots = pick.shape[0]
    tokens, width = rows.shape
    tile = width // 2
    out_spec = pl.BlockSpec((slots, tile), lambda i: (0, i))
    return pl.pallas_call(
        pick_more_kernel if found else pick_kernel,
        out_shape=jax.ShapeDtypeStruct((slots, width), bf16),
        grid=(width // tile,),
        in_specs=[
            pl.BlockSpec((slots, tokens), lambda i: (0, half)),
            pl.BlockSpec((tokens, tile), lambda i: (0, i)),
        ]
        + [out_spec] * len(found),
        out_specs=out_spec,
        compiler_params=pltpu.CompilerParams(vmem_limit_bytes=32 * 2**20),
        cost_estimate=pl.CostEstimate(
            flops=2 * slots * tokens * width, bytes_accessed=5 * 10**6, transcendentals=0
        ),
        name="pick_rows",
    )(pick, rows, *found)


def merge_kernel(merge_ref, rows_ref, out_ref):
    out_ref[...] = mm(merge_ref[...], rows_ref[...]).astype(bf16)


def merge_rows(merge, half, rows):
    tokens, slots = merge.shape
    width = rows.shape[1]
    return pl.pallas_call(
        merge_kernel,
        out_shape=jax.ShapeDtypeStruct((tokens // 2, width), bf16),
        grid=(1,),
        in_specs=[
            pl.BlockSpec((tokens // 2, slots), lambda i: (half, 0)),
            pl.BlockSpec((slots, width), lambda i: (0, 0)),
        ],
        out_specs=pl.BlockSpec((tokens // 2, width), lambda i: (0, 0)),
        compiler_params=pltpu.CompilerParams(vmem_limit_bytes=32 * 2**20),
        cost_estimate=pl.CostEstimate(
            flops=tokens * slots * width, bytes_accessed=5 * 10**6, transcendentals=0
        ),
        name="merge_rows",
    )(merge, rows)


def swap_cores(array):
    return lax.ppermute(array, "local", [(i, i ^ 1) for i in range(LOCAL)])


def across_chips(array):
    groups = [[side + 2 * chip for chip in range(LOCAL // 2)] for side in range(2)]
    return lax.all_to_all(
        array, "local", split_axis=0, concat_axis=0, tiled=True, axis_index_groups=groups
    )


def along_row(array):
    nodes = lax.axis_size("node")
    groups = [[row + z for z in range(NODE_ROW)] for row in range(0, nodes, NODE_ROW)]
    return lax.all_to_all(
        array, "node", split_axis=0, concat_axis=0, tiled=True, axis_index_groups=groups
    )


def across_rows(array):
    nodes = lax.axis_size("node")
    groups = [[row + z for row in range(0, nodes, NODE_ROW)] for z in range(NODE_ROW)]
    return lax.all_to_all(
        array, "node", split_axis=0, concat_axis=0, tiled=True, axis_index_groups=groups
    )


def across_nodes(array):
    return lax.all_to_all(array, "node", split_axis=0, concat_axis=0, tiled=True)


def local(
    hidden_in, queries, key_vectors, values, out_gate, log_decay, write_rate, norm_gain,
    out_weight, post_gain, expert_index, route_weight, expert_gate_up, expert_down,
):
    node_count = lax.axis_size("node")
    local_index = lax.axis_index("local")
    side = local_index % 2
    tokens, top = expert_index.shape
    chips = LOCAL // 2
    share = tokens // LOCAL
    width = hidden_in.shape[1]
    capacity = 6 * tokens * top // (5 * node_count * LOCAL)
    side_array = side.astype(jnp.int32).reshape(1)

    def by_side(array):
        split = array.T.reshape(top, chips, 2, share)
        split = jnp.where(side == 0, split, split[:, :, ::-1])
        return split.transpose(0, 2, 1, 3).reshape(top, tokens)

    pick, merge = routing(
        local_index.astype(jnp.int32).reshape(1), by_side(expert_index), by_side(route_weight),
        node_count, capacity,
    )

    payload, cum, inner, value_rows, starts = shard_maps(key_vectors, values, log_decay.T, write_rate.T)
    maps = along_row(payload)
    core, reach = block_reads(queries, key_vectors, cum, inner, value_rows, starts)
    maps, core, reach, pick, merge = lax.optimization_barrier((maps, core, reach, pick, merge))
    totals = across_rows(row_total(maps, node_count // NODE_ROW))
    row = (lax.axis_index("node") // NODE_ROW).astype(jnp.int32).reshape(1)
    carried = along_row(shard_starts(row, totals, maps)).reshape(HEADS * DV, DK)
    own_half, other_part = gated_part(
        side_array, core, reach, carried, out_gate, norm_gain.reshape(1, DV), out_weight
    )
    partial = project(own_half, out_weight, swap_cores(other_part))
    parts = across_chips(partial.reshape(chips, share, width))
    hidden_state, normed = residual(parts, hidden_in, post_gain.reshape(1, width))
    own_rows = across_chips(normed).reshape(chips * share, width)
    other_rows = swap_cores(own_rows)
    found = pick_rows(pick, 0, own_rows)
    rows = pick_rows(pick, 1, other_rows, found).reshape(node_count, capacity, width)
    rows = across_nodes(rows).reshape(node_count * capacity, width)
    gate_up = jnp.dot(rows, expert_gate_up[0], preferred_element_type=f32)
    half_width = gate_up.shape[1] // 2
    hidden_rows = (jax.nn.silu(gate_up[:, :half_width]) * gate_up[:, half_width:]).astype(bf16)
    results = jnp.dot(hidden_rows, expert_down[0], preferred_element_type=f32).astype(bf16)
    returned = across_nodes(results.reshape(node_count, capacity, width)).reshape(
        node_count * capacity, width
    )
    given = swap_cores(merge_rows(merge, 1, returned))
    kept = merge_rows(merge, 0, returned)
    summed = (kept.astype(f32) + given.astype(f32)).astype(bf16)
    arrived = across_chips(summed.reshape(chips, share, width))
    return finish(arrived, hidden_state)


def solution(mesh):
    return jax.shard_map(
        local,
        mesh=mesh,
        in_specs=(
            P(("node", "local"), None),
            P("node", "local"),
            P("node", "local"),
            P("node", "local"),
            P("node", "local"),
            P("node", "local"),
            P("node", "local"),
            P(),
            P("local", None),
            P(),
            P("node", None),
            P("node", None),
            P(("node", "local"), None, None),
            P(("node", "local"), None, None),
        ),
        out_specs=P(("node", "local"), None),
        check_vma=False,
    )
```
